256 devices in a mesh: blk: 256 (over y, x, z, core).
Axes of the slice: x: 4, y: 4, z: 8, core: 2. Of those that a mesh axis runs over, the one named last changes fastest.
Arguments:
- image_emb: bfloat16 [32768, 1152], P('blk'), may hold values from -0.59765625 to 0.59765625
- image_ids: int32 [32768], P('blk'), may hold values from 0 to 127
- text_feats: bfloat16 [32768, 1152], P('blk'), may hold values from -0.59765625 to 0.59765625
- text_ids: int32 [32768], P('blk'), may hold values from 0 to 127
- text_head: bfloat16 [1152, 1152], replicated, may hold values from -0.099609375 to 1.5
Outputs:
- grad_image: bfloat16 [32768, 1152], P('blk')
- grad_text: bfloat16 [32768, 1152], P('blk')
- grad_head: float32 [1152, 1152], replicated
The draws below stay inside these ranges and needn't reach their ends.
All inputs are finite; a program needn't handle non-finite values.
Results may differ from the reference program's by a relative error of at most 0.0038.
The reference program's roundings to bfloat16 on the way (of `text_z`, `image_z`, `coef` and `grad_pre`) count: a program that leaves them out, or rounds other values in their place, can miss the bound.
Values may be sent and summed in bfloat16 or wider, within the bound.
A program may use at most 64 MiB of HBM per device.

```python
import jax
import jax.numpy as jnp
from jax import lax

D = 1152
IMG_DEV = 128
TXT_DEV = 128
REACH = 6
IMAGES = 32768
TEXTS = 32768
N_BLK = 256


def pair_tables(key):
    key = jax.random.fold_in(key, 907)
    image_pairs = jax.random.randint(jax.random.fold_in(key, 1), (IMAGES,), 0, TXT_DEV, dtype=jnp.int32)
    text_pairs = jax.random.randint(jax.random.fold_in(key, 2), (TEXTS,), 0, TXT_DEV, dtype=jnp.int32)
    latent = jax.random.normal(jax.random.fold_in(key, 3), (TXT_DEV, D), jnp.float32)
    topics = jax.random.normal(jax.random.fold_in(key, 4), (16, D), jnp.float32)
    return (image_pairs, text_pairs, latent, topics)


def mixed_rows(key, pair_ids, jitter, latent, topics, topic_weight, low_scale, high_scale):
    key_weight, key_scale = jax.random.split(key)
    row_count = pair_ids.shape[0]
    weights = jax.random.uniform(key_weight, (row_count, 1), jnp.float32, 0.4, 1.4)
    scales = jnp.exp(jax.random.uniform(key_scale, (row_count, 1), jnp.float32, jnp.log(low_scale), jnp.log(high_scale)))
    signal = weights * latent[pair_ids] + topic_weight * topics[pair_ids % 16]
    return jnp.clip((signal + jitter) * scales, -0.59765625, 0.59765625)


def draw_image_ids(key, part):
    image_pairs, text_pairs, latent, topics = pair_tables(key)
    return image_pairs


def draw_text_ids(key, part):
    image_pairs, text_pairs, latent, topics = pair_tables(key)
    return text_pairs


def draw_image_emb(key, part):
    image_pairs, text_pairs, latent, topics = pair_tables(key)
    key = jax.random.fold_in(key, 11)
    key_jitter, key_rows = jax.random.split(key)
    jitter = jax.random.normal(key_jitter, (IMAGES, D), jnp.float32)
    values = mixed_rows(key_rows, image_pairs, jitter, latent, topics, 0.7, 0.01, 0.1)
    return values.astype(jnp.bfloat16)


def draw_text_feats(key, part):
    image_pairs, text_pairs, latent, topics = pair_tables(key)
    key = jax.random.fold_in(key, 23)
    key_jitter, key_rows = jax.random.split(key)
    jitter = jax.random.normal(key_jitter, (TEXTS, D), jnp.float32)
    values = mixed_rows(key_rows, text_pairs, jitter, latent, topics, 0.7, 0.01, 0.1)
    return values.astype(jnp.bfloat16)


def draw_text_head(key, part):
    key = jax.random.fold_in(key, 37)
    key_diagonal, key_spread = jax.random.split(key)
    diagonal = jax.random.uniform(key_diagonal, (D,), jnp.float32, 0.6, 1.4)
    spread = jax.random.normal(key_spread, (D, D), jnp.float32)
    matrix = jnp.eye(D, dtype=jnp.float32) * diagonal[None, :] + 0.5 * spread * D ** (-0.5)
    return jnp.clip(matrix, -0.099609375, 1.5).astype(jnp.bfloat16)


def setup_inputs(seed: int = 0) -> dict:
    key_list = jax.random.split(jax.random.key(seed), 6)
    return {
        "image_emb": draw_image_emb(jax.random.fold_in(key_list[5], 71), 0),
        "image_ids": draw_image_ids(jax.random.fold_in(key_list[5], 71), 0),
        "text_feats": draw_text_feats(jax.random.fold_in(key_list[5], 71), 0),
        "text_ids": draw_text_ids(jax.random.fold_in(key_list[5], 71), 0),
        "text_head": draw_text_head(jax.random.fold_in(key_list[5], 71), 0),
    }


def reference(image_emb, image_ids, text_feats, text_ids, text_head):
    pre = jnp.dot(text_feats, text_head, preferred_element_type=jnp.float32)
    text_inv = lax.rsqrt(lax.optimization_barrier(jnp.sum(pre * pre, axis=-1, keepdims=True)) + 1e-06)
    text_unit = pre * text_inv
    text_z = text_unit.astype(jnp.bfloat16)
    image_f = image_emb.astype(jnp.float32)
    image_inv = lax.rsqrt(lax.optimization_barrier(jnp.sum(image_f * image_f, axis=-1, keepdims=True)) + 1e-06)
    image_unit = image_f * image_inv
    image_z = image_unit.astype(jnp.bfloat16)
    blocks = N_BLK
    iz_blocks = image_z.reshape(blocks, IMG_DEV, D).astype(jnp.float32)
    tz_blocks = text_z.reshape(blocks, TXT_DEV, D).astype(jnp.float32)
    img_idb = image_ids.reshape(blocks, IMG_DEV)
    txt_idb = text_ids.reshape(blocks, TXT_DEV)
    grad_iz = jnp.zeros((blocks, IMG_DEV, D), jnp.float32)
    grad_tz = jnp.zeros((blocks, TXT_DEV, D), jnp.float32)
    for offset in range(-(REACH - 1), REACH + 1):
        tz_roll = jnp.roll(tz_blocks, offset, axis=0)
        id_roll = jnp.roll(txt_idb, offset, axis=0)
        logit = 10.0 * jnp.einsum('bid,btd->bit', iz_blocks, tz_roll) - 5.0
        label = jnp.where(img_idb[:, :, None] == id_roll[:, None, :], 1.0, -1.0).astype(jnp.float32)
        coef = (-label * jax.nn.sigmoid(-label * logit)).astype(jnp.bfloat16).astype(jnp.float32)
        grad_iz = grad_iz + 10.0 * jnp.einsum('bit,btd->bid', coef, tz_roll)
        term = 10.0 * jnp.einsum('bit,bid->btd', coef, iz_blocks)
        grad_tz = grad_tz + jnp.roll(term, -offset, axis=0)
    grad_iz = grad_iz.reshape(IMAGES, D)
    grad_tz = grad_tz.reshape(TEXTS, D)
    grad_image = ((grad_iz - image_unit * lax.optimization_barrier(jnp.sum(image_unit * grad_iz, axis=-1, keepdims=True))) * image_inv).astype(jnp.bfloat16)
    grad_pre = ((grad_tz - text_unit * lax.optimization_barrier(jnp.sum(text_unit * grad_tz, axis=-1, keepdims=True))) * text_inv).astype(jnp.bfloat16)
    grad_text = jnp.dot(grad_pre, text_head.T, preferred_element_type=jnp.float32).astype(jnp.bfloat16)
    grad_head = jnp.dot(text_feats.T, grad_pre, preferred_element_type=jnp.float32)
    return (grad_image, grad_text, grad_head)
```

```python
import jax
import jax.numpy as jnp
from jax import lax
from jax.experimental import pallas as pl
from jax.experimental.pallas import tpu as pltpu
from jax.sharding import PartitionSpec as P

MESH = pl.DeviceIdType.MESH
D = 1152
B = 128
REACH = 6
SLICE = 80
XR = 96
OWNER = (0, 4, 8, 12, 2, 3, 7, 11, 15)
X_LANES = ((0, 384), (640, 256))
Y_LANES = ((384, 256), (896, 256))
NT = (((1,), (1,)), ((), ()))


def start_row(p):
    return pl.multiple_of(16 * ((9 * p) // 2), 16)


def kernel(
    img_ref, imgid_ref, txt_ref, txtid_ref, head_ref,
    gimg_ref, gtxt_ref, g_ref,
    imgs, txts, img_pair, txt_pair, ids, img_col, txt_col, acc_t, acc_i, got_t, got_i,
    pre, gp_t, feats, gp_in, part, sums, block,
    band_s, band_r, id_s, id_r, pair_s, pair_r, fa_s, fa_r, gp_s, gp_r, rs_s, rs_r, az_s, az_r,
    a2_s, a2_r, a3_s, a3_r, am_s, am_r,
):
    me = lax.axis_index("blk")
    core = lax.rem(me, 2)
    q = lax.rem(me, 16)
    z = q // 2
    p = me // 16
    x = lax.rem(p, 4)
    y = p // 4
    mate = me + 1 - 2 * core
    right, left = lax.rem(me + 2, 256), lax.rem(me + 254, 256)

    def at(y2, x2):
        return (y2 * 4 + x2) * 16 + q

    xp, xm = lax.rem(x + 1, 4), lax.rem(x + 3, 4)
    yp, ym = lax.rem(y + 1, 4), lax.rem(y + 3, 4)

    barrier = pltpu.get_barrier_semaphore()

    def greet(device):
        pl.semaphore_signal(barrier, inc=1, device_id=(device,), device_id_type=MESH)

    for step in (2, 4, 6, 250, 252, 254):
        greet(lax.rem(me + step, 256))

    def greet_group(i, carry):
        greet(lax.rem(p + i, 16) * 16 + q)
        greet(p * 16 + lax.rem(q + i, 16))
        return carry

    lax.fori_loop(1, 16, greet_group, 0)

    sent = []

    def copy(src, dst, ssem, rsem, device):
        return pltpu.make_async_remote_copy(
            src_ref=src, dst_ref=dst, send_sem=ssem, recv_sem=rsem,
            device_id=(device,), device_id_type=MESH,
        )

    def send(src, dst, ssem, rsem, device):
        c = copy(src, dst, ssem, rsem, device)
        c.start()
        sent.append(c)
        return c

    image_f = img_ref[...].astype(jnp.float32)
    image_inv = lax.rsqrt(jnp.sum(image_f * image_f, axis=-1, keepdims=True) + 1e-06)
    own_z = (image_f * image_inv).astype(jnp.bfloat16)
    imgs[0, 0] = own_z
    img_pair[0:B] = own_z
    ids[0] = jnp.concatenate(
        [
            jnp.broadcast_to(imgid_ref[...], (8, B)),
            jnp.broadcast_to(txtid_ref[...], (8, B)),
        ],
        axis=0,
    )
    feats[y, x] = txt_ref[...]

    pl.semaphore_wait(barrier, 36)

    H = B // 2

    def band_send(kind, buf, step, way, half):
        rows = pl.ds(half * H, H)
        src = buf.at[0, 0, rows] if step == 1 else buf.at[step - 1, way, rows]
        k = ((kind * 2 + way) * 3 + step - 1) * 2 + half
        return send(
            src, buf.at[step, way, rows], band_s.at[k], band_r.at[k], (right, left)[way]
        )

    hold = {}

    def band_start(kind, buf):
        for half in range(2):
            for way in range(2):
                hold[kind, 1, way, half] = band_send(kind, buf, 1, way, half)

    def band_forward(kind, buf, step):
        for half in range(2):
            for way in range(2):
                hold[kind, step, way, half].wait_recv()
                if step < 3:
                    hold[kind, step + 1, way, half] = band_send(kind, buf, step + 1, way, half)

    band_start(0, imgs)
    id_copies = []
    for n, step in enumerate((2, 4, 6)):
        for way in range(2):
            k = 2 * n + way
            to = lax.rem(me + (step if way == 0 else 256 - step), 256)
            id_copies.append(send(ids.at[0], ids.at[1 + k], id_s.at[k], id_r.at[k], to))
    id_copies.append(send(ids.at[0], ids.at[7], id_s.at[6], id_r.at[6], mate))
    img_mate = send(imgs.at[0, 0], img_pair.at[pl.ds(B, B)], pair_s.at[0], pair_r.at[0], mate)

    HX = XR // 2
    YR = B - XR
    HY = YR // 2
    own = feats.at[y, x]
    rx, ry = pl.ds(0, XR), pl.ds(XR, YR)
    f_sem = [0]

    def feat_send(src, device):
        k = f_sem[0]
        f_sem[0] += 1
        return send(src, src, fa_s.at[k], fa_r.at[k], device)

    fa1 = [
        feat_send(feats.at[y, x, rx], at(y, xp)),
        feat_send(feats.at[y, x, rx], at(y, xm)),
        feat_send(feats.at[y, x, ry], at(yp, x)),
        feat_send(feats.at[y, x, ry], at(ym, x)),
    ]

    def feats_second():
        for c in fa1:
            c.wait_recv()
        return [
            feat_send(feats.at[y, xm, pl.ds(0, HX)], at(y, xp)),
            feat_send(feats.at[y, xp, pl.ds(HX, HX)], at(y, xm)),
            feat_send(feats.at[ym, x, pl.ds(XR, HY)], at(yp, x)),
            feat_send(feats.at[yp, x, pl.ds(XR + HY, HY)], at(ym, x)),
        ]

    def feats_third(prev):
        for c in prev:
            c.wait_recv()
        return [
            feat_send(feats.at[y, :, rx], at(yp, x)),
            feat_send(feats.at[y, :, rx], at(ym, x)),
            feat_send(feats.at[:, x, ry], at(y, xp)),
            feat_send(feats.at[:, x, ry], at(y, xm)),
        ]

    def feats_fourth(prev):
        for c in prev:
            c.wait_recv()
        return [
            feat_send(feats.at[ym, :, pl.ds(0, HX)], at(yp, x)),
            feat_send(feats.at[yp, :, pl.ds(HX, HX)], at(ym, x)),
            feat_send(feats.at[:, xm, pl.ds(XR, HY)], at(y, xp)),
            feat_send(feats.at[:, xp, pl.ds(XR + HY, HY)], at(y, xm)),
        ]

    pre[...] = jnp.dot(txt_ref[...], head_ref[...], preferred_element_type=jnp.float32)
    text_pre = pre[...]
    text_inv = lax.rsqrt(jnp.sum(text_pre * text_pre, axis=-1, keepdims=True) + 1e-06)
    text_z = (text_pre * text_inv).astype(jnp.bfloat16)
    txts[0, 0] = text_z
    txt_pair[0:B] = text_z
    txt_mate = send(txts.at[0, 0], txt_pair.at[pl.ds(B, B)], pair_s.at[1], pair_r.at[1], mate)

    for c in id_copies:
        c.wait_recv()

    def column(row):
        return jnp.transpose(jnp.broadcast_to(row.astype(jnp.float32), (B, B)))

    for h, slot in ((0, 0), (1, 7)):
        img_col[pl.ds(h * B, B)] = column(ids[slot, 0:1])
        txt_col[pl.ds(h * B, B)] = column(ids[slot, 8:9])

    def process(kind, step, here_ref, col_ref, blocks, acc_ref):
        slots = (0,) if step == 0 else (2 * step - 1, 2 * step)
        logit = (
            10.0 * lax.dot_general(here_ref[...], blocks, NT, preferred_element_type=jnp.float32)
            - 5.0
        )
        coefs = []
        for n, slot in enumerate(slots):
            row = ids[slot, 8 * kind : 8 * kind + 1].astype(jnp.float32)
            label = jnp.where(col_ref[...] == row, 1.0, -1.0)
            part_logit = logit[:, n * B : (n + 1) * B]
            coef = -label * jax.nn.sigmoid(-label * part_logit)
            if step == 3:
                delta = 2 * step * (2 * n - 1)
                offset = (delta, delta + 2 * core - 1) if kind == 0 else (-delta, 1 - 2 * core - delta)
                keep = [
                    jnp.where((o >= 1 - REACH) & (o <= REACH), 1.0, 0.0).astype(jnp.float32)
                    for o in offset
                ]
                half = lax.broadcasted_iota(jnp.int32, coef.shape, 0) < B
                coef = coef * jnp.where(half, keep[0], keep[1])
            coefs.append(coef.astype(jnp.bfloat16))
        coef = coefs[0] if len(coefs) == 1 else jnp.concatenate(coefs, axis=1)
        term = jnp.dot(coef, blocks, preferred_element_type=jnp.float32)
        if step == 0:
            acc_ref[...] = term
        else:
            acc_ref[...] += term

    def pair_block(buf, step):
        return buf[step].reshape(2 * B, D)

    txt_mate.wait_recv()
    process(0, 0, txt_pair, txt_col, imgs[0, 0], acc_t)
    band_forward(0, imgs, 1)
    fa2 = feats_second()
    process(0, 1, txt_pair, txt_col, pair_block(imgs, 1), acc_t)
    band_forward(0, imgs, 2)
    band_start(1, txts)
    fa3 = feats_third(fa2)
    process(0, 2, txt_pair, txt_col, pair_block(imgs, 2), acc_t)
    img_mate.wait_recv()
    process(1, 0, img_pair, img_col, txts[0, 0], acc_i)
    band_forward(0, imgs, 3)
    process(0, 3, txt_pair, txt_col, pair_block(imgs, 3), acc_t)
    swap = send(acc_t.at[pl.ds(B, B)], got_t, pair_s.at[2], pair_r.at[2], mate)
    swap.wait_recv()
    grad_tz = 10.0 * (acc_t[0:B] + got_t[...])
    text_unit = pre[...] * text_inv
    grad_pre = (
        grad_tz - text_unit * jnp.sum(text_unit * grad_tz, axis=-1, keepdims=True)
    ) * text_inv
    for n in range(9):
        gp_t[n * B : (n + 1) * B] = jnp.transpose(grad_pre[:, n * B : (n + 1) * B]).astype(
            jnp.bfloat16
        )
    grad_pre = grad_pre.astype(jnp.bfloat16)

    def gp_copy(i):
        p2 = lax.rem(p + i, 16)
        return copy(
            gp_t.at[pl.ds(start_row(p2), SLICE)],
            gp_in.at[:, pl.ds(pl.multiple_of(p * B, B), B)],
            gp_s.at[i], gp_r.at[i], p2 * 16 + q,
        )

    def gp_send(i, carry):
        gp_copy(i).start()
        return carry

    lax.fori_loop(1, 16, gp_send, 0)
    gp_in[:, pl.ds(pl.multiple_of(p * B, B), B)] = gp_t[pl.ds(start_row(p), SLICE)]

    band_forward(1, txts, 1)
    fa4 = feats_fourth(fa3)
    process(1, 1, img_pair, img_col, pair_block(txts, 1), acc_i)
    gtxt_ref[...] = lax.dot_general(
        grad_pre, head_ref[...], NT, preferred_element_type=jnp.float32
    ).astype(jnp.bfloat16)
    band_forward(1, txts, 2)

    for c in fa4:
        c.wait_recv()

    def gp_wait(i, carry):
        gp_copy(i).wait_recv()
        return carry

    lax.fori_loop(1, 16, gp_wait, 0)
    slices = jnp.dot(gp_in[...], feats[...].reshape(16 * B, D), preferred_element_type=jnp.float32)
    for n in range(9):
        part[n] = slices[:, n * B : (n + 1) * B]

    def rs_copy(n, to):
        return copy(part.at[n], sums.at[q], rs_s.at[n], rs_r.at[q], p * 16 + to)

    for n, to in enumerate(OWNER):
        @pl.when(q != to)
        def _():
            rs_copy(n, to).start()

        @pl.when(q == to)
        def _():
            sums[q] = part[n]

    process(1, 2, img_pair, img_col, pair_block(txts, 2), acc_i)

    mine = jnp.where(core == 0, jnp.where(q == 2, 4, z // 2), 5 + z // 2)
    is_owner = jnp.logical_or(lax.rem(z, 2) == core, q == 2)
    lanes = pl.ds(pl.multiple_of(mine * B, B), B)

    def az_copy(i):
        z2 = lax.rem(z + i, 8)
        return copy(
            block, g_ref.at[y, x, :, lanes], az_s.at[i], az_r.at[mine], p * 16 + 2 * z2 + core
        )

    @pl.when(is_owner)
    def _():
        def rs_wait(i, carry):
            q2 = lax.rem(q + i, 16)
            copy(part.at[0], sums.at[q2], rs_s.at[0], rs_r.at[q2], mate).wait_recv()
            return carry

        lax.fori_loop(1, 16, rs_wait, 0)
        total = sums[0]
        for n in range(1, 16):
            total = total + sums[n]
        block[...] = total.astype(jnp.bfloat16)
        g_ref[y, x, :, lanes] = total.astype(jnp.bfloat16)

        def az_send(i, carry):
            az_copy(i).start()
            return carry

        lax.fori_loop(1, 8, az_send, 0)

    band_forward(1, txts, 3)
    process(1, 3, img_pair, img_col, pair_block(txts, 3), acc_i)
    swap_i = send(acc_i.at[pl.ds(B, B)], got_i, pair_s.at[3], pair_r.at[3], mate)

    def finish_image():
        swap_i.wait_recv()
        grad_iz = 10.0 * (acc_i[0:B] + got_i[...])
        image_g = img_ref[...].astype(jnp.float32)
        image_unit = image_g * image_inv
        gimg_ref[...] = (
            (grad_iz - image_unit * jnp.sum(image_unit * grad_iz, axis=-1, keepdims=True))
            * image_inv
        ).astype(jnp.bfloat16)

    def gather(cc):
        first, count = ((0, 5), (5, 4))[cc]
        for n in range(first, first + count):
            @pl.when(q != OWNER[n])
            def _():
                copy(
                    block, g_ref.at[y, x, :, pl.ds(n * B, B)], az_s.at[0], az_r.at[n], mate
                ).wait_recv()
        lx, ly = pl.ds(*X_LANES[cc]), pl.ds(*Y_LANES[cc])

        def mate_copy(k, view):
            return copy(view, view, am_s.at[k], am_r.at[k], mate)

        second = []
        for i in (1, 3, 2):
            x2, y2 = lax.rem(x + i, 4), lax.rem(y + i, 4)
            vx, vy = g_ref.at[y, x, :, lx], g_ref.at[y, x, :, ly]
            second.append(copy(vx, vx, a2_s.at[i], a2_r.at[i], at(y, x2)))
            second.append(copy(vy, vy, a2_s.at[4 + i], a2_r.at[4 + i], at(y2, x)))
        for c in second:
            c.start()
        finish_image()
        for c in second:
            c.wait_recv()
        third = []
        for i in (1, 3, 2):
            x2, y2 = lax.rem(x + i, 4), lax.rem(y + i, 4)
            vx, vy = g_ref.at[y, :, :, lx], g_ref.at[:, x, :, ly]
            third.append((i, copy(vx, vx, a3_s.at[i], a3_r.at[i], at(y2, x)),
                          copy(vy, vy, a3_s.at[4 + i], a3_r.at[4 + i], at(y, x2))))
        for i, a, b in third:
            a.start()
            b.start()
        mates = [mate_copy(0, g_ref.at[y, :, :, lx]), mate_copy(4, g_ref.at[:, x, :, ly])]
        for c in mates:
            c.start()
        for i, a, b in third:
            a.wait_recv()
            c = mate_copy(i, g_ref.at[lax.rem(y + 4 - i, 4), :, :, lx])
            c.start()
            mates.append(c)
            b.wait_recv()
            c = mate_copy(4 + i, g_ref.at[:, lax.rem(x + 4 - i, 4), :, ly])
            c.start()
            mates.append(c)
        for c in second:
            c.wait_send()
        for i, a, b in third:
            a.wait_send()
            b.wait_send()
        for c in mates:
            c.wait_send()
        other = 1 - cc
        ox, oy = pl.ds(*X_LANES[other]), pl.ds(*Y_LANES[other])
        for i in range(4):
            mate_copy(i, g_ref.at[lax.rem(y + 4 - i, 4), :, :, ox]).wait_recv()
            mate_copy(4 + i, g_ref.at[:, lax.rem(x + 4 - i, 4), :, oy]).wait_recv()

    for cc in range(2):
        @pl.when(core == cc)
        def _():
            gather(cc)

    for c in sent:
        c.wait_send()

    def gp_drain(i, carry):
        gp_copy(i).wait_send()
        return carry

    lax.fori_loop(1, 16, gp_drain, 0)
    for n, to in enumerate(OWNER):
        @pl.when(q != to)
        def _():
            rs_copy(n, to).wait_send()

    @pl.when(is_owner)
    def _():
        def az_drain(i, carry):
            az_copy(i).wait_send()
            return carry

        lax.fori_loop(1, 8, az_drain, 0)


def finish(g_ref, gimg_ref, gtxt_ref, oimg_ref, otxt_ref, ohead_ref, whole):
    @pl.when(pl.program_id(0) == 0)
    def _():
        oimg_ref[...] = gimg_ref[...]
        otxt_ref[...] = gtxt_ref[...]
        for p in range(16):
            if p % 2 == 0:
                whole[72 * p : 72 * p + 80] = g_ref[p // 4, p % 4]
            else:
                whole[72 * p + 8 : 72 * p + 72] = g_ref[p // 4, p % 4, 16:80]

    n = pl.program_id(0)
    eye = (
        lax.broadcasted_iota(jnp.int32, (B, B), 0) == lax.broadcasted_iota(jnp.int32, (B, B), 1)
    ).astype(jnp.bfloat16)
    ohead_ref[...] = lax.dot_general(
        eye, whole[:, pl.ds(pl.multiple_of(n * B, B), B)], NT, preferred_element_type=jnp.float32
    )


def shards(image_emb, image_ids, text_feats, text_ids, text_head):
    bf, f32 = jnp.bfloat16, jnp.float32
    vmem = pl.BlockSpec(memory_space=pltpu.VMEM)
    dma = pltpu.SemaphoreType.DMA
    scratch = [
        pltpu.VMEM((4, 2, B, D), bf),
        pltpu.VMEM((4, 2, B, D), bf),
        pltpu.VMEM((2 * B, D), bf),
        pltpu.VMEM((2 * B, D), bf),
        pltpu.VMEM((8, 16, B), jnp.int32),
        pltpu.VMEM((2 * B, B), f32),
        pltpu.VMEM((2 * B, B), f32),
        pltpu.VMEM((2 * B, D), f32),
        pltpu.VMEM((2 * B, D), f32),
        pltpu.VMEM((B, D), f32),
        pltpu.VMEM((B, D), f32),
        pltpu.VMEM((B, D), f32),
        pltpu.VMEM((D, B), bf),
        pltpu.VMEM((4, 4, B, D), bf),
        pltpu.VMEM((SLICE, 16 * B), bf),
        pltpu.VMEM((9, SLICE, B), f32),
        pltpu.VMEM((16, SLICE, B), f32),
        pltpu.VMEM((SLICE, B), bf),
    ]
    for n in (24, 7, 4, 16, 16):
        scratch += [dma((n,)), dma((n,))]
    scratch += [dma((9,)), dma((16,)), dma((8,)), dma((9,))]
    for n in (8, 8, 8):
        scratch += [dma((n,)), dma((n,))]
    gimg, gtxt, g = pl.pallas_call(
        kernel,
        out_shape=(
            jax.ShapeDtypeStruct((B, D), bf),
            jax.ShapeDtypeStruct((B, D), bf),
            jax.ShapeDtypeStruct((4, 4, SLICE, D), bf),
        ),
        in_specs=[vmem] * 5,
        out_specs=(vmem, vmem, vmem),
        scratch_shapes=scratch,
        compiler_params=pltpu.CompilerParams(
            collective_id=0, has_side_effects=True, vmem_limit_bytes=48 * 2**20
        ),
    )(image_emb, image_ids.reshape(1, B), text_feats, text_ids.reshape(1, B), text_head)
    fixed = pl.BlockSpec((B, D), lambda n: (0, 0))
    return pl.pallas_call(
        finish,
        grid=(9,),
        out_shape=(
            jax.ShapeDtypeStruct((B, D), bf),
            jax.ShapeDtypeStruct((B, D), bf),
            jax.ShapeDtypeStruct((D, D), f32),
        ),
        in_specs=[pl.BlockSpec((4, 4, SLICE, D), lambda n: (0, 0, 0, 0)), fixed, fixed],
        out_specs=(fixed, fixed, pl.BlockSpec((B, D), lambda n: (n, 0))),
        scratch_shapes=[pltpu.VMEM((D, D), bf)],
        compiler_params=pltpu.CompilerParams(vmem_limit_bytes=32 * 2**20),
    )(g, gimg, gtxt)


def solution(mesh):
    placed = (P("blk", None), P("blk"), P("blk", None), P("blk"), P())
    return jax.shard_map(
        shards,
        mesh=mesh,
        in_specs=placed,
        out_specs=(P("blk", None), P("blk", None), P()),
        check_vma=False,
    )
```

```python
import jax
import jax.numpy as jnp
from jax import lax
from jax.experimental import pallas as pl
from jax.experimental.pallas import tpu as pltpu
from jax.sharding import PartitionSpec as P

MESH = pl.DeviceIdType.MESH
D = 1152
B = 128
REACH = 6
SLICE = 80
OWNER = (0, 4, 8, 12, 2, 3, 7, 11, 15)
X_LANES = ((256, 384), (640, 256))
X_ALL = (256, 640)
WIDE = 384
NT = (((1,), (1,)), ((), ()))


def start_row(a):
    return pl.multiple_of(16 * ((9 * a) // 2), 16)


def kernel(
    img_hbm, imgid_ref, txt_hbm, txtid_ref, head_hbm,
    gimg_ref, gtxt_ref, g_ref,
    img_ref, txt_ref, head_ref, imgs, txts, img_pair, txt_pair, ids, img_col, txt_col,
    acc_t, acc_i, got_t, got_i, pre, gp_t, feats, gp_in, part, sums, block,
    load, band_s, band_r, id_s, id_r, pair_s, pair_r, f_s, f_r, gp_s, gp_r, rs_s, rs_r,
    az_s, az_r, a2_s, a2_r, a3_s, a3_r, am_s, am_r,
):
    loads = [
        pltpu.make_async_copy(a, b, load.at[n])
        for n, (a, b) in enumerate(
            ((img_hbm, img_ref), (txt_hbm, txt_ref), (head_hbm, head_ref))
        )
    ]
    for c in loads:
        c.start()

    me = lax.axis_index("blk")
    core = lax.rem(me, 2)
    z = lax.rem(me // 2, 8)
    x = lax.rem(me // 16, 4)
    y = me // 64
    g, xp = x // 2, lax.rem(x, 2)
    a = (y * 2 + xp) * 2 + core
    b = z * 2 + g

    def at(y2, x2, z2, c2):
        return ((y2 * 4 + x2) * 8 + z2) * 2 + c2

    def of_group(a2):
        return at(a2 // 4, 2 * g + lax.rem(a2 // 2, 2), z, lax.rem(a2, 2))

    def of_column(b2):
        return at(y, 2 * lax.rem(b2, 2) + xp, b2 // 2, core)

    mate = at(y, x, z, 1 - core)
    partner = at(y, x + 1 - 2 * xp, z, core)
    right, left = lax.rem(me + 2, 256), lax.rem(me + 254, 256)
    yp, ym, yo = lax.rem(y + 1, 4), lax.rem(y + 3, 4), lax.rem(y + 2, 4)
    up, down = at(yp, x, z, core), at(ym, x, z, core)

    barrier = pltpu.get_barrier_semaphore()

    def greet(device):
        pl.semaphore_signal(barrier, inc=1, device_id=(device,), device_id_type=MESH)

    for step in (2, 4, 6, 250, 252, 254):
        greet(lax.rem(me + step, 256))
    greet(at(y, 3 - x, z, core))

    def greet_groups(i, carry):
        greet(of_group(lax.rem(a + i, 16)))
        greet(of_column(lax.rem(b + i, 16)))
        return carry

    lax.fori_loop(1, 16, greet_groups, 0)

    sent = []

    def copy(src, dst, ssem, rsem, device):
        return pltpu.make_async_remote_copy(
            src_ref=src, dst_ref=dst, send_sem=ssem, recv_sem=rsem,
            device_id=(device,), device_id_type=MESH,
        )

    def send(src, dst, ssem, rsem, device):
        c = copy(src, dst, ssem, rsem, device)
        c.start()
        sent.append(c)
        return c

    loads[0].wait()
    image_f = img_ref[...].astype(jnp.float32)
    image_inv = lax.rsqrt(jnp.sum(image_f * image_f, axis=-1, keepdims=True) + 1e-06)
    own_z = (image_f * image_inv).astype(jnp.bfloat16)
    imgs[0, 0] = own_z
    img_pair[0:B] = own_z
    ids[0] = jnp.concatenate(
        [
            jnp.broadcast_to(imgid_ref[...], (8, B)),
            jnp.broadcast_to(txtid_ref[...], (8, B)),
        ],
        axis=0,
    )
    loads[1].wait()
    feats[y, xp, core] = txt_ref[...]
    loads[2].wait()
    pre[...] = jnp.dot(txt_ref[...], head_ref[...], preferred_element_type=jnp.float32)
    text_pre = pre[...]
    text_inv = lax.rsqrt(jnp.sum(text_pre * text_pre, axis=-1, keepdims=True) + 1e-06)
    text_z = (text_pre * text_inv).astype(jnp.bfloat16)
    txts[0, 0] = text_z
    txt_pair[0:B] = text_z

    pl.semaphore_wait(barrier, 37)

    H = B // 2
    hold = {}

    def band_send(kind, buf, step, way, half):
        rows = pl.ds(half * H, H)
        src = buf.at[0, 0, rows] if step == 1 else buf.at[step - 1, way, rows]
        k = ((kind * 2 + way) * 3 + step - 1) * 2 + half
        hold[kind, step, way, half] = send(
            src, buf.at[step, way, rows], band_s.at[k], band_r.at[k], (right, left)[way]
        )

    def band_start(kind, buf):
        for half in range(2):
            for way in range(2):
                band_send(kind, buf, 1, way, half)

    def band_forward(kind, buf, step):
        for half in range(2):
            for way in range(2):
                hold[kind, step, way, half].wait_recv()
                if step < 3:
                    band_send(kind, buf, step + 1, way, half)

    def band_wait(kind, step):
        for half in range(2):
            for way in range(2):
                hold[kind, step, way, half].wait_recv()

    def band_pass(kind, buf, step):
        for half in range(2):
            for way in range(2):
                band_send(kind, buf, step + 1, way, half)

    band_start(0, imgs)
    txt_mate = send(txts.at[0, 0], txt_pair.at[pl.ds(B, B)], pair_s.at[1], pair_r.at[1], mate)
    id_copies = [send(ids.at[0], ids.at[7], id_s.at[6], id_r.at[6], mate)]
    for n, step in enumerate((2, 4, 6)):
        for way in range(2):
            k = 2 * n + way
            to = lax.rem(me + (step if way == 0 else 256 - step), 256)
            id_copies.append(send(ids.at[0], ids.at[1 + k], id_s.at[k], id_r.at[k], to))

    F = {}

    def feat_send(name, k, y2, xp2, device, rows=pl.ds(0, B)):
        view = feats.at[y2, xp2, core, rows]
        F[name] = send(view, view, f_s.at[k], f_r.at[k], device)

    low, high = pl.ds(0, H), pl.ds(H, H)
    other = 1 - xp
    feat_send("x", 0, y, xp, partner)
    feat_send("u", 1, y, xp, up)
    feat_send("d", 2, y, xp, down)
    img_mate = send(imgs.at[0, 0], img_pair.at[pl.ds(B, B)], pair_s.at[0], pair_r.at[0], mate)
    feat_send("m0", 8 + 0, y, xp, mate)

    def feats_second():
        F["x"].wait_recv()
        feat_send("xu", 3, y, other, up)
        feat_send("xd", 4, y, other, down)
        F["u"].wait_recv()
        feat_send("uu", 5, ym, xp, up, low)
        F["d"].wait_recv()
        feat_send("dd", 6, yp, xp, down, high)
        feat_send("m1", 8 + 1, y, other, mate)
        feat_send("m2", 8 + 2, ym, xp, mate)
        feat_send("m3", 8 + 3, yp, xp, mate)

    def feats_third():
        F["xu"].wait_recv()
        feat_send("xuu", 7, ym, other, up, low)
        F["xd"].wait_recv()
        feat_send("xdd", 16, yp, other, down, high)
        feat_send("m4", 8 + 4, ym, other, mate)
        feat_send("m5", 8 + 5, yp, other, mate)
        F["uu"].wait_recv()
        F["dd"].wait_recv()
        feat_send("m6", 8 + 6, yo, xp, mate)

    def feats_fourth():
        F["xuu"].wait_recv()
        F["xdd"].wait_recv()
        feat_send("m7", 8 + 7, yo, other, mate)

    def feats_wait():
        for n in range(8):
            F["m%d" % n].wait_recv()

    for c in id_copies:
        c.wait_recv()

    def column(row):
        return jnp.transpose(jnp.broadcast_to(row.astype(jnp.float32), (B, B)))

    for h, slot in ((0, 0), (1, 7)):
        img_col[pl.ds(h * B, B)] = column(ids[slot, 0:1])
        txt_col[pl.ds(h * B, B)] = column(ids[slot, 8:9])

    def process(kind, step, here_ref, col_ref, blocks, acc_ref):
        slots = (0,) if step == 0 else (2 * step - 1, 2 * step)
        logit = (
            10.0 * lax.dot_general(here_ref[...], blocks, NT, preferred_element_type=jnp.float32)
            - 5.0
        )
        coefs = []
        for n, slot in enumerate(slots):
            row = ids[slot, 8 * kind : 8 * kind + 1].astype(jnp.float32)
            label = jnp.where(col_ref[...] == row, 1.0, -1.0)
            part_logit = logit[:, n * B : (n + 1) * B]
            coef = -label * jax.nn.sigmoid(-label * part_logit)
            if step == 3:
                delta = 2 * step * (2 * n - 1)
                offset = (delta, delta + 2 * core - 1) if kind == 0 else (-delta, 1 - 2 * core - delta)
                keep = [
                    jnp.where((o >= 1 - REACH) & (o <= REACH), 1.0, 0.0).astype(jnp.float32)
                    for o in offset
                ]
                half = lax.broadcasted_iota(jnp.int32, coef.shape, 0) < B
                coef = coef * jnp.where(half, keep[0], keep[1])
            coefs.append(coef.astype(jnp.bfloat16))
        coef = coefs[0] if len(coefs) == 1 else jnp.concatenate(coefs, axis=1)
        term = jnp.dot(coef, blocks, preferred_element_type=jnp.float32)
        if step == 0:
            acc_ref[...] = term
        else:
            acc_ref[...] += term

    def pair_block(buf, step):
        return buf[step].reshape(2 * B, D)

    def process_images(step):
        process(0, step, txt_pair, txt_col, pair_block(imgs, step), acc_t)

    def process_texts(step):
        process(1, step, img_pair, img_col, pair_block(txts, step), acc_i)

    txt_mate.wait_recv()
    process(0, 0, txt_pair, txt_col, imgs[0, 0], acc_t)
    img_mate.wait_recv()
    process(1, 0, img_pair, img_col, txts[0, 0], acc_i)
    band_forward(0, imgs, 1)
    feats_second()
    process_images(1)
    band_forward(0, imgs, 2)
    band_start(1, txts)
    feats_third()
    process_images(2)
    band_wait(0, 3)
    process_images(3)
    swap = send(acc_t.at[pl.ds(B, B)], got_t, pair_s.at[2], pair_r.at[2], mate)
    text_unit = pre[...] * text_inv
    swap.wait_recv()
    grad_tz = 10.0 * (acc_t[0:B] + got_t[...])
    grad_pre = (
        grad_tz - text_unit * jnp.sum(text_unit * grad_tz, axis=-1, keepdims=True)
    ) * text_inv
    for n in range(9):
        gp_t[n * B : (n + 1) * B] = jnp.transpose(grad_pre[:, n * B : (n + 1) * B]).astype(
            jnp.bfloat16
        )
    grad_pre = grad_pre.astype(jnp.bfloat16)

    def gp_copy(i):
        a2 = lax.rem(a + i, 16)
        return copy(
            gp_t.at[pl.ds(start_row(a2), SLICE)],
            gp_in.at[:, pl.ds(pl.multiple_of(a * B, B), B)],
            gp_s.at[i], gp_r.at[i], of_group(a2),
        )

    def gp_send(i, carry):
        gp_copy(i).start()
        return carry

    lax.fori_loop(1, 16, gp_send, 0)
    gp_in[:, pl.ds(pl.multiple_of(a * B, B), B)] = gp_t[pl.ds(start_row(a), SLICE)]
    feats_fourth()
    gtxt_ref[...] = lax.dot_general(
        grad_pre, head_ref[...], NT, preferred_element_type=jnp.float32
    ).astype(jnp.bfloat16)
    band_forward(1, txts, 1)
    process_texts(1)
    feats_wait()

    def gp_wait(i, carry):
        gp_copy(i).wait_recv()
        return carry

    lax.fori_loop(1, 16, gp_wait, 0)
    slices = jnp.dot(gp_in[...], feats[...].reshape(16 * B, D), preferred_element_type=jnp.float32)
    for n in range(9):
        part[n] = slices[:, n * B : (n + 1) * B]

    def rs_copy(n, to):
        return copy(part.at[n], sums.at[b], rs_s.at[n], rs_r.at[b], of_column(to))

    for n, to in enumerate(OWNER):
        @pl.when(b != to)
        def _():
            rs_copy(n, to).start()

        @pl.when(b == to)
        def _():
            sums[b] = part[n]

    band_wait(1, 2)
    process_texts(2)

    mine = jnp.where(g == 0, jnp.where(b == 2, 4, z // 2), 5 + z // 2)
    is_owner = jnp.logical_or(lax.rem(z, 2) == g, b == 2)
    lanes = pl.ds(pl.multiple_of(mine * B, B), B)

    def az_copy(i):
        return copy(
            block, g_ref.at[y, xp, core, :, lanes], az_s.at[i], az_r.at[mine],
            at(y, x, lax.rem(z + i, 8), core),
        )

    def own_block():
        return pltpu.make_async_copy(block, g_ref.at[y, xp, core, :, lanes], load.at[0])

    @pl.when(is_owner)
    def _():
        def rs_wait(i, carry):
            b2 = lax.rem(b + i, 16)
            copy(part.at[0], sums.at[b2], rs_s.at[0], rs_r.at[b2], mate).wait_recv()
            return carry

        lax.fori_loop(1, 16, rs_wait, 0)
        total = sums[0]
        for n in range(1, 16):
            total = total + sums[n]
        block[...] = total.astype(jnp.bfloat16)

        def az_send(i, carry):
            az_copy(i).start()
            return carry

        lax.fori_loop(1, 8, az_send, 0)
        own_block().start()
        own_block().wait()

    for gg, (first, count) in enumerate(((0, 5), (5, 4))):
        for n in range(first, first + count):
            @pl.when((g == gg) & (b != OWNER[n]))
            def _():
                copy(
                    block, g_ref.at[y, xp, core, :, pl.ds(n * B, B)], az_s.at[0], az_r.at[n], mate
                ).wait_recv()

    def lanes_y(g2):
        return pl.ds(pl.multiple_of(896 * g2, B), 256)

    def back(x2, i):
        return lax.rem(x2 + 4 - i, 4)

    def along_x(i):
        return at(y, lax.rem(x + i, 4), z, core)

    def along_y(i):
        return at(lax.rem(y + i, 4), x, z, core)

    def second_x(i, gg):
        view = g_ref.at[y, xp, core, :, pl.ds(*X_LANES[gg])]
        return copy(view, view, a2_s.at[i], a2_r.at[i], along_x(i))

    def second_y(i):
        view = g_ref.at[y, xp, core, :, lanes_y(g)]
        return copy(view, view, a2_s.at[4 + i], a2_r.at[4 + i], along_y(i))

    def third_x(i):
        view = g_ref.at[y, :, core, :, pl.ds(*X_ALL)]
        return copy(view, view, a3_s.at[i], a3_r.at[i], along_y(i))

    def third_y(i):
        view = g_ref.at[:, xp, core, :, lanes_y(g)]
        return copy(view, view, a3_s.at[4 + i], a3_r.at[4 + i], along_x(i))

    def mate_x(i, c2):
        view = g_ref.at[back(y, i), :, c2, :, pl.ds(*X_ALL)]
        return copy(view, view, am_s.at[i], am_r.at[i], mate)

    def mate_y(i, c2):
        x2 = back(x, i)
        view = g_ref.at[:, lax.rem(x2, 2), c2, :, lanes_y(x2 // 2)]
        return copy(view, view, am_s.at[4 + i], am_r.at[4 + i], mate)

    ORDER = (1, 3, 2)
    for i in ORDER:
        for gg in range(2):
            @pl.when(g == gg)
            def _():
                second_x(i, gg).start()
        second_y(i).start()
    band_pass(1, txts, 2)
    for i in ORDER:
        for gg in range(2):
            @pl.when(back(x, i) // 2 == gg)
            def _():
                second_x(i, gg).wait_recv()
    for i in ORDER:
        third_x(i).start()
    for i in ORDER:
        second_y(i).wait_recv()
    for i in ORDER:
        third_y(i).start()
    mate_x(0, core).start()
    mate_y(0, core).start()

    band_wait(1, 3)
    process_texts(3)
    swap_i = send(acc_i.at[pl.ds(B, B)], got_i, pair_s.at[3], pair_r.at[3], mate)
    swap_i.wait_recv()
    grad_iz = 10.0 * (acc_i[0:B] + got_i[...])
    image_g = img_ref[...].astype(jnp.float32)
    image_unit = image_g * image_inv
    gimg_ref[...] = (
        (grad_iz - image_unit * jnp.sum(image_unit * grad_iz, axis=-1, keepdims=True)) * image_inv
    ).astype(jnp.bfloat16)

    for i in ORDER:
        third_x(i).wait_recv()
        mate_x(i, core).start()
        third_y(i).wait_recv()
        mate_y(i, core).start()

    for c in sent:
        c.wait_send()

    def gp_drain(i, carry):
        gp_copy(i).wait_send()
        return carry

    lax.fori_loop(1, 16, gp_drain, 0)
    for n, to in enumerate(OWNER):
        @pl.when(b != to)
        def _():
            rs_copy(n, to).wait_send()

    @pl.when(is_owner)
    def _():
        def az_drain(i, carry):
            az_copy(i).wait_send()
            return carry

        lax.fori_loop(1, 8, az_drain, 0)

    for i in ORDER:
        for gg in range(2):
            @pl.when(g == gg)
            def _():
                second_x(i, gg).wait_send()
        second_y(i).wait_send()
        third_x(i).wait_send()
        third_y(i).wait_send()
    for i in range(4):
        mate_x(i, core).wait_send()
        mate_y(i, core).wait_send()
        mate_x(i, 1 - core).wait_recv()
        mate_y(i, 1 - core).wait_recv()


def finish(g_ref, gimg_ref, gtxt_ref, oimg_ref, otxt_ref, ohead_ref, whole):
    @pl.when(pl.program_id(0) == 0)
    def _():
        oimg_ref[...] = gimg_ref[...]
        otxt_ref[...] = gtxt_ref[...]

    for a in range(16):
        view = g_ref[a // 4, (a // 2) % 2, a % 2]
        if a % 2 == 0:
            whole[72 * a : 72 * a + 80] = view
        else:
            whole[72 * a + 8 : 72 * a + 72] = view[16:80]
    eye = (
        lax.broadcasted_iota(jnp.int32, (B, B), 0) == lax.broadcasted_iota(jnp.int32, (B, B), 1)
    ).astype(jnp.bfloat16)
    for n in range(WIDE // B):
        ohead_ref[n * B : (n + 1) * B] = lax.dot_general(
            eye, whole[:, n * B : (n + 1) * B], NT, preferred_element_type=jnp.float32
        )


def shards(image_emb, image_ids, text_feats, text_ids, text_head):
    bf, f32 = jnp.bfloat16, jnp.float32
    vmem = pl.BlockSpec(memory_space=pltpu.VMEM)
    hbm = pl.BlockSpec(memory_space=pl.ANY)
    dma = pltpu.SemaphoreType.DMA
    scratch = [
        pltpu.VMEM((B, D), bf),
        pltpu.VMEM((B, D), bf),
        pltpu.VMEM((D, D), bf),
        pltpu.VMEM((4, 2, B, D), bf),
        pltpu.VMEM((4, 2, B, D), bf),
        pltpu.VMEM((2 * B, D), bf),
        pltpu.VMEM((2 * B, D), bf),
        pltpu.VMEM((8, 16, B), jnp.int32),
        pltpu.VMEM((2 * B, B), f32),
        pltpu.VMEM((2 * B, B), f32),
        pltpu.VMEM((2 * B, D), f32),
        pltpu.VMEM((2 * B, D), f32),
        pltpu.VMEM((B, D), f32),
        pltpu.VMEM((B, D), f32),
        pltpu.VMEM((B, D), f32),
        pltpu.VMEM((D, B), bf),
        pltpu.VMEM((4, 2, 2, B, D), bf),
        pltpu.VMEM((SLICE, 16 * B), bf),
        pltpu.VMEM((9, SLICE, B), f32),
        pltpu.VMEM((16, SLICE, B), f32),
        pltpu.VMEM((SLICE, B), bf),
        dma((3,)),
    ]
    for n in (24, 7, 4, 17, 16):
        scratch += [dma((n,)), dma((n,))]
    scratch += [dma((9,)), dma((16,)), dma((8,)), dma((9,))]
    for n in (8, 8, 8):
        scratch += [dma((n,)), dma((n,))]
    gimg, gtxt, g = pl.pallas_call(
        kernel,
        out_shape=(
            jax.ShapeDtypeStruct((B, D), bf),
            jax.ShapeDtypeStruct((B, D), bf),
            jax.ShapeDtypeStruct((4, 2, 2, SLICE, D), bf),
        ),
        in_specs=[hbm, vmem, hbm, vmem, hbm],
        out_specs=(vmem, vmem, hbm),
        scratch_shapes=scratch,
        compiler_params=pltpu.CompilerParams(
            collective_id=0, has_side_effects=True, vmem_limit_bytes=60 * 2**20
        ),
    )(image_emb, image_ids.reshape(1, B), text_feats, text_ids.reshape(1, B), text_head)
    fixed = pl.BlockSpec((B, D), lambda n: (0, 0))
    return pl.pallas_call(
        finish,
        grid=(D // WIDE,),
        out_shape=(
            jax.ShapeDtypeStruct((B, D), bf),
            jax.ShapeDtypeStruct((B, D), bf),
            jax.ShapeDtypeStruct((D, D), f32),
        ),
        in_specs=[pl.BlockSpec((4, 2, 2, SLICE, WIDE), lambda n: (0, 0, 0, 0, n)), fixed, fixed],
        out_specs=(fixed, fixed, pl.BlockSpec((WIDE, D), lambda n: (n, 0))),
        scratch_shapes=[pltpu.VMEM((D, WIDE), bf)],
        compiler_params=pltpu.CompilerParams(vmem_limit_bytes=60 * 2**20),
    )(g, gimg, gtxt)


def solution(mesh):
    placed = (P("blk", None), P("blk"), P("blk", None), P("blk"), P())
    return jax.shard_map(
        shards,
        mesh=mesh,
        in_specs=placed,
        out_specs=(P("blk", None), P("blk", None), P()),
        check_vma=False,
    )
```

```python
import jax
import jax.numpy as jnp
from jax import lax
from jax.experimental import pallas as pl
from jax.experimental.pallas import tpu as pltpu
from jax.sharding import PartitionSpec as P

MESH = pl.DeviceIdType.MESH
D = 1152
B = 128
REACH = 6
SLICE = 80
OWNER = (0, 4, 8, 12, 2, 3, 7, 11, 15)
X_LANES = ((256, 384), (640, 256))
X_ALL = (256, 640)
WIDE = 384
NT = (((1,), (1,)), ((), ()))


def start_row(a):
    return pl.multiple_of(16 * ((9 * a) // 2), 16)


def kernel(
    img_hbm, imgid_ref, txt_hbm, txtid_ref, head_hbm,
    gimg_ref, gtxt_ref, g_ref,
    img_ref, txt_ref, head_ref, imgs, txts, img_pair, txt_pair, ids, img_col, txt_col,
    acc_t, acc_i, got_t, got_i, pre, gp_t, feats, gp_in, part, sums, block,
    load, band_s, band_r, id_s, id_r, pair_s, pair_r, f_s, f_r, gp_s, gp_r, rs_s, rs_r,
    az_s, az_r, a2_s, a2_r, a3_s, a3_r, am_s, am_r, g_vm, keep,
):
    loads = [
        pltpu.make_async_copy(a, b, load.at[n])
        for n, (a, b) in enumerate(
            ((img_hbm, img_ref), (txt_hbm, txt_ref), (head_hbm, head_ref))
        )
    ]
    for c in loads:
        c.start()

    me = lax.axis_index("blk")
    core = lax.rem(me, 2)
    z = lax.rem(me // 2, 8)
    x = lax.rem(me // 16, 4)
    y = me // 64
    g, xp = x // 2, lax.rem(x, 2)
    a = (y * 2 + xp) * 2 + core
    b = z * 2 + g

    def at(y2, x2, z2, c2):
        return ((y2 * 4 + x2) * 8 + z2) * 2 + c2

    def of_group(a2):
        return at(a2 // 4, 2 * g + lax.rem(a2 // 2, 2), z, lax.rem(a2, 2))

    def of_column(b2):
        return at(y, 2 * lax.rem(b2, 2) + xp, b2 // 2, core)

    mate = at(y, x, z, 1 - core)
    partner = at(y, x + 1 - 2 * xp, z, core)
    right, left = lax.rem(me + 2, 256), lax.rem(me + 254, 256)
    yp, ym, yo = lax.rem(y + 1, 4), lax.rem(y + 3, 4), lax.rem(y + 2, 4)
    up, down = at(yp, x, z, core), at(ym, x, z, core)

    barrier = pltpu.get_barrier_semaphore()

    def greet(device):
        pl.semaphore_signal(barrier, inc=1, device_id=(device,), device_id_type=MESH)

    for step in (2, 4, 6, 250, 252, 254):
        greet(lax.rem(me + step, 256))
    greet(at(y, 3 - x, z, core))

    def greet_groups(i, carry):
        greet(of_group(lax.rem(a + i, 16)))
        greet(of_column(lax.rem(b + i, 16)))
        return carry

    lax.fori_loop(1, 16, greet_groups, 0)

    sent = []

    def copy(src, dst, ssem, rsem, device):
        return pltpu.make_async_remote_copy(
            src_ref=src, dst_ref=dst, send_sem=ssem, recv_sem=rsem,
            device_id=(device,), device_id_type=MESH,
        )

    def send(src, dst, ssem, rsem, device):
        c = copy(src, dst, ssem, rsem, device)
        c.start()
        sent.append(c)
        return c

    loads[0].wait()
    image_f = img_ref[...].astype(jnp.float32)
    image_inv = lax.rsqrt(jnp.sum(image_f * image_f, axis=-1, keepdims=True) + 1e-06)
    own_z = (image_f * image_inv).astype(jnp.bfloat16)
    imgs[0, 0] = own_z
    img_pair[0:B] = own_z
    ids[0] = jnp.concatenate(
        [
            jnp.broadcast_to(imgid_ref[...], (8, B)),
            jnp.broadcast_to(txtid_ref[...], (8, B)),
        ],
        axis=0,
    )
    loads[1].wait()
    feats[y, xp, core] = txt_ref[...]
    loads[2].wait()
    pre[...] = jnp.dot(txt_ref[...], head_ref[...], preferred_element_type=jnp.float32)
    text_pre = pre[...]
    text_inv = lax.rsqrt(jnp.sum(text_pre * text_pre, axis=-1, keepdims=True) + 1e-06)
    text_z = (text_pre * text_inv).astype(jnp.bfloat16)
    txts[0, 0] = text_z
    txt_pair[0:B] = text_z

    @pl.when(core == 0)
    def _():
        imgs[3, 0] = jnp.zeros((B, D), jnp.bfloat16)

    @pl.when(core == 1)
    def _():
        txts[3, 1] = jnp.zeros((B, D), jnp.bfloat16)

    pl.semaphore_wait(barrier, 37)

    hold = {}
    PARTS = (4, 2)

    def idle(kind, step, way):
        return step == 3 and way == kind

    def wanted(kind):
        return core == 1 if kind == 0 else core == 0

    def band_copy(kind, buf, step, way, n):
        rows = pl.ds(n * (B // PARTS[kind]), B // PARTS[kind])
        src = buf.at[0, 0, rows] if step == 1 else buf.at[step - 1, way, rows]
        k = ((kind * 2 + way) * 3 + step - 1) * 4 + n
        return copy(src, buf.at[step, way, rows], band_s.at[k], band_r.at[k], (right, left)[way])

    def band_send(kind, buf, step, way, n):
        if idle(kind, step, way):
            @pl.when(wanted(kind))
            def _():
                band_copy(kind, buf, step, way, n).start()
            return
        c = band_copy(kind, buf, step, way, n)
        c.start()
        sent.append(c)
        hold[kind, step, way, n] = c

    def band_start(kind, buf, first, last):
        for n in range(first, last):
            for way in range(2):
                band_send(kind, buf, 1, way, n)

    def band_pace(n):
        for way in range(2):
            c = hold[0, 1, way, n]
            c.wait_send()
            sent.remove(c)
            band_send(0, imgs, 1, way, n + 2)

    def band_forward(kind, buf, step):
        for n in range(PARTS[kind]):
            for way in range(2):
                hold[kind, step, way, n].wait_recv()
                band_send(kind, buf, step + 1, way, n)

    def band_wait(kind, buf, step):
        for n in range(PARTS[kind]):
            for way in range(2):
                if idle(kind, step, way):
                    @pl.when(wanted(kind))
                    def _():
                        band_copy(kind, buf, step, way, n).wait_recv()
                else:
                    hold[kind, step, way, n].wait_recv()

    band_start(0, imgs, 0, 2)
    txt_mate = send(txts.at[0, 0], txt_pair.at[pl.ds(B, B)], pair_s.at[1], pair_r.at[1], mate)
    id_copies = [send(ids.at[0], ids.at[7], id_s.at[6], id_r.at[6], mate)]
    for n, step in enumerate((2, 4, 6)):
        for way in range(2):
            k = 2 * n + way
            to = lax.rem(me + (step if way == 0 else 256 - step), 256)
            id_copies.append(send(ids.at[0], ids.at[1 + k], id_s.at[k], id_r.at[k], to))

    F = {}

    def feat_send(name, k, y2, xp2, device):
        view = feats.at[y2, xp2, core]
        F[name] = send(view, view, f_s.at[k], f_r.at[k], device)

    other = 1 - xp
    feat_send("x", 0, y, xp, partner)
    feat_send("u", 1, y, xp, up)
    feat_send("d", 2, y, xp, down)
    img_mate = send(imgs.at[0, 0], img_pair.at[pl.ds(B, B)], pair_s.at[0], pair_r.at[0], mate)
    feat_send("m0", 8 + 0, y, xp, mate)

    over = jnp.where(g == 0, yp, ym)
    across = jnp.where(g == 0, down, up)

    def feats_second():
        F["x"].wait_recv()
        feat_send("xu", 3, y, other, up)
        feat_send("xd", 4, y, other, down)
        F["u"].wait_recv()
        F["d"].wait_recv()
        feat_send("o", 5, over, xp, across)
        feat_send("m1", 8 + 1, y, other, mate)
        feat_send("m2", 8 + 2, ym, xp, mate)
        feat_send("m3", 8 + 3, yp, xp, mate)

    def feats_third():
        F["xu"].wait_recv()
        F["xd"].wait_recv()
        feat_send("xo", 6, over, other, across)
        feat_send("m4", 8 + 4, ym, other, mate)
        feat_send("m5", 8 + 5, yp, other, mate)
        F["o"].wait_recv()
        feat_send("m6", 8 + 6, yo, xp, mate)

    def feats_fourth():
        F["xo"].wait_recv()
        feat_send("m7", 8 + 7, yo, other, mate)

    def feats_wait():
        for n in range(8):
            F["m%d" % n].wait_recv()

    for c in id_copies:
        c.wait_recv()

    def column(row):
        return jnp.transpose(jnp.broadcast_to(row.astype(jnp.float32), (B, B)))

    for h, slot in ((0, 0), (1, 7)):
        img_col[pl.ds(h * B, B)] = column(ids[slot, 0:1])
        txt_col[pl.ds(h * B, B)] = column(ids[slot, 8:9])

    def process(kind, step, here_ref, col_ref, blocks, acc_ref):
        slots = (0,) if step == 0 else (2 * step - 1, 2 * step)
        logit = (
            10.0 * lax.dot_general(here_ref[...], blocks, NT, preferred_element_type=jnp.float32)
            - 5.0
        )
        coefs = []
        for n, slot in enumerate(slots):
            row = ids[slot, 8 * kind : 8 * kind + 1].astype(jnp.float32)
            label = jnp.where(col_ref[...] == row, 1.0, -1.0)
            part_logit = logit[:, n * B : (n + 1) * B]
            coef = -label * jax.nn.sigmoid(-label * part_logit)
            if step == 3:
                delta = 2 * step * (2 * n - 1)
                offset = (delta, delta + 2 * core - 1) if kind == 0 else (-delta, 1 - 2 * core - delta)
                keep = [
                    jnp.where((o >= 1 - REACH) & (o <= REACH), 1.0, 0.0).astype(jnp.float32)
                    for o in offset
                ]
                half = lax.broadcasted_iota(jnp.int32, coef.shape, 0) < B
                coef = coef * jnp.where(half, keep[0], keep[1])
            coefs.append(coef.astype(jnp.bfloat16))
        coef = coefs[0] if len(coefs) == 1 else jnp.concatenate(coefs, axis=1)
        term = jnp.dot(coef, blocks, preferred_element_type=jnp.float32)
        if step == 0:
            acc_ref[...] = term
        else:
            acc_ref[...] += term

    def pair_block(buf, step):
        return buf[step].reshape(2 * B, D)

    def process_images(step):
        process(0, step, txt_pair, txt_col, pair_block(imgs, step), acc_t)

    def process_texts(step):
        process(1, step, img_pair, img_col, pair_block(txts, step), acc_i)

    band_pace(0)
    txt_mate.wait_recv()
    process(0, 0, txt_pair, txt_col, imgs[0, 0], acc_t)
    band_pace(1)
    img_mate.wait_recv()
    process(1, 0, img_pair, img_col, txts[0, 0], acc_i)
    band_forward(0, imgs, 1)
    feats_second()
    process_images(1)
    band_forward(0, imgs, 2)
    feats_third()
    process_images(2)
    band_wait(0, imgs, 3)
    band_start(1, txts, 0, 2)
    process_images(3)
    swap = send(acc_t.at[pl.ds(B, B)], got_t, pair_s.at[2], pair_r.at[2], mate)
    text_unit = pre[...] * text_inv
    swap.wait_recv()
    grad_tz = 10.0 * (acc_t[0:B] + got_t[...])
    grad_pre = (
        grad_tz - text_unit * jnp.sum(text_unit * grad_tz, axis=-1, keepdims=True)
    ) * text_inv
    for n in range(9):
        gp_t[n * B : (n + 1) * B] = jnp.transpose(grad_pre[:, n * B : (n + 1) * B]).astype(
            jnp.bfloat16
        )
    grad_pre = grad_pre.astype(jnp.bfloat16)

    def gp_copy(i):
        a2 = lax.rem(a + i, 16)
        return copy(
            gp_t.at[pl.ds(start_row(a2), SLICE)],
            gp_in.at[:, pl.ds(pl.multiple_of(a * B, B), B)],
            gp_s.at[i], gp_r.at[i], of_group(a2),
        )

    def gp_send(i, carry):
        gp_copy(i).start()
        return carry

    lax.fori_loop(1, 16, gp_send, 0)
    gp_in[:, pl.ds(pl.multiple_of(a * B, B), B)] = gp_t[pl.ds(start_row(a), SLICE)]
    feats_fourth()
    gtxt_ref[...] = lax.dot_general(
        grad_pre, head_ref[...], NT, preferred_element_type=jnp.float32
    ).astype(jnp.bfloat16)
    band_forward(1, txts, 1)
    process_texts(1)
    feats_wait()

    def gp_wait(i, carry):
        gp_copy(i).wait_recv()
        return carry

    lax.fori_loop(1, 16, gp_wait, 0)
    slices = jnp.dot(gp_in[...], feats[...].reshape(16 * B, D), preferred_element_type=jnp.float32)
    for n in range(9):
        part[n] = slices[:, n * B : (n + 1) * B]

    def rs_copy(n, to):
        return copy(part.at[n], sums.at[b], rs_s.at[n], rs_r.at[b], of_column(to))

    for n, to in enumerate(OWNER):
        @pl.when(b != to)
        def _():
            rs_copy(n, to).start()

        @pl.when(b == to)
        def _():
            sums[b] = part[n]

    band_forward(1, txts, 2)
    process_texts(2)
    mine = jnp.where(g == 0, jnp.where(b == 2, 4, z // 2), 5 + z // 2)
    is_owner = jnp.logical_or(lax.rem(z, 2) == g, b == 2)
    lanes = pl.ds(pl.multiple_of(mine * B, B), B)

    def az_copy(i):
        return copy(
            block, g_vm.at[y, xp, core, :, lanes], az_s.at[i], az_r.at[mine],
            at(y, x, lax.rem(z + i, 8), core),
        )

    @pl.when(is_owner)
    def _():
        def rs_wait(i, carry):
            b2 = lax.rem(b + i, 16)
            copy(part.at[0], sums.at[b2], rs_s.at[0], rs_r.at[b2], mate).wait_recv()
            return carry

        lax.fori_loop(1, 16, rs_wait, 0)
        total = sums[0]
        for n in range(1, 16):
            total = total + sums[n]
        block[...] = total.astype(jnp.bfloat16)
        g_vm[y, xp, core, :, lanes] = total.astype(jnp.bfloat16)

        def az_send(i, carry):
            az_copy(i).start()
            return carry

        lax.fori_loop(1, 8, az_send, 0)

    for gg, (first, count) in enumerate(((0, 5), (5, 4))):
        for n in range(first, first + count):
            @pl.when((g == gg) & (b != OWNER[n]))
            def _():
                copy(
                    block, g_vm.at[y, xp, core, :, pl.ds(n * B, B)], az_s.at[0], az_r.at[n], mate
                ).wait_recv()

    def lanes_y(g2):
        return pl.ds(pl.multiple_of(896 * g2, B), 256)

    def back(x2, i):
        return lax.rem(x2 + 4 - i, 4)

    def along_x(i):
        return at(y, lax.rem(x + i, 4), z, core)

    def along_y(i):
        return at(lax.rem(y + i, 4), x, z, core)

    def second_x(i, gg):
        view = g_vm.at[y, xp, core, :, pl.ds(*X_LANES[gg])]
        return copy(view, view, a2_s.at[i], a2_r.at[i], along_x(i))

    def second_y(i):
        view = g_vm.at[y, xp, core, :, lanes_y(g)]
        return copy(view, view, a2_s.at[4 + i], a2_r.at[4 + i], along_y(i))

    def third_x(i):
        view = g_vm.at[y, :, core, :, pl.ds(*X_ALL)]
        return copy(view, view, a3_s.at[i], a3_r.at[i], along_y(i))

    def third_y(i):
        view = g_vm.at[:, xp, core, :, lanes_y(g)]
        return copy(view, view, a3_s.at[4 + i], a3_r.at[4 + i], along_x(i))

    def place_x(ref, i, c2):
        return ref.at[back(y, i), :, c2, :, pl.ds(*X_ALL)]

    def place_y(ref, i, c2):
        x2 = back(x, i)
        return ref.at[:, lax.rem(x2, 2), c2, :, lanes_y(x2 // 2)]

    def mate_x(i, c2):
        return copy(place_x(g_vm, i, c2), place_x(g_ref, i, c2), am_s.at[i], am_r.at[i], mate)

    def mate_y(i, c2):
        return copy(
            place_y(g_vm, i, c2), place_y(g_ref, i, c2), am_s.at[4 + i], am_r.at[4 + i], mate
        )

    def keep_x(i):
        return pltpu.make_async_copy(place_x(g_vm, i, core), place_x(g_ref, i, core), keep.at[i])

    def keep_y(i):
        return pltpu.make_async_copy(
            place_y(g_vm, i, core), place_y(g_ref, i, core), keep.at[4 + i]
        )

    ORDER = (1, 3, 2)
    for i in ORDER:
        for gg in range(2):
            @pl.when(g == gg)
            def _():
                second_x(i, gg).start()
        second_y(i).start()
    for i in ORDER:
        for gg in range(2):
            @pl.when(back(x, i) // 2 == gg)
            def _():
                second_x(i, gg).wait_recv()
    for i in ORDER:
        third_x(i).start()
    for i in ORDER:
        second_y(i).wait_recv()
    for i in ORDER:
        third_y(i).start()
    mate_x(0, core).start()
    keep_x(0).start()
    mate_y(0, core).start()
    keep_y(0).start()


    band_wait(1, txts, 3)
    process_texts(3)
    swap_i = send(acc_i.at[pl.ds(B, B)], got_i, pair_s.at[3], pair_r.at[3], mate)
    third_x(1).wait_recv()
    mate_x(1, core).start()
    keep_x(1).start()
    third_y(1).wait_recv()
    mate_y(1, core).start()
    keep_y(1).start()
    third_x(3).wait_recv()
    mate_x(3, core).start()
    keep_x(3).start()
    third_y(3).wait_recv()
    mate_y(3, core).start()
    keep_y(3).start()
    third_x(2).wait_recv()
    mate_x(2, core).start()
    keep_x(2).start()
    third_y(2).wait_recv()
    mate_y(2, core).start()
    keep_y(2).start()
    swap_i.wait_recv()
    grad_iz = 10.0 * (acc_i[0:B] + got_i[...])
    image_g = img_ref[...].astype(jnp.float32)
    image_unit = image_g * image_inv
    gimg_ref[...] = (
        (grad_iz - image_unit * jnp.sum(image_unit * grad_iz, axis=-1, keepdims=True)) * image_inv
    ).astype(jnp.bfloat16)

    for kind, buf in ((0, imgs), (1, txts)):
        @pl.when(wanted(kind))
        def _():
            for n in range(PARTS[kind]):
                band_copy(kind, buf, 3, kind, n).wait_send()
    for c in sent:
        c.wait_send()

    def gp_drain(i, carry):
        gp_copy(i).wait_send()
        return carry

    lax.fori_loop(1, 16, gp_drain, 0)
    for n, to in enumerate(OWNER):
        @pl.when(b != to)
        def _():
            rs_copy(n, to).wait_send()

    @pl.when(is_owner)
    def _():
        def az_drain(i, carry):
            az_copy(i).wait_send()
            return carry

        lax.fori_loop(1, 8, az_drain, 0)

    for i in ORDER:
        for gg in range(2):
            @pl.when(g == gg)
            def _():
                second_x(i, gg).wait_send()
        second_y(i).wait_send()
        third_x(i).wait_send()
        third_y(i).wait_send()
    for i in range(4):
        keep_x(i).wait()
        keep_y(i).wait()
        mate_x(i, core).wait_send()
        mate_y(i, core).wait_send()
        mate_x(i, 1 - core).wait_recv()
        mate_y(i, 1 - core).wait_recv()


def finish(g_ref, gimg_ref, gtxt_ref, oimg_ref, otxt_ref, ohead_ref, whole):
    @pl.when(pl.program_id(0) == 0)
    def _():
        oimg_ref[...] = gimg_ref[...]
        otxt_ref[...] = gtxt_ref[...]

    for a in range(16):
        view = g_ref[a // 4, (a // 2) % 2, a % 2]
        if a % 2 == 0:
            whole[72 * a : 72 * a + 80] = view
        else:
            whole[72 * a + 8 : 72 * a + 72] = view[16:80]
    for start, size in ((0, 256), (256, 128)):
        eye = lax.broadcasted_iota(jnp.int32, (size, size), 0) == lax.broadcasted_iota(
            jnp.int32, (size, size), 1
        )
        ohead_ref[start : start + size] = lax.dot_general(
            eye.astype(jnp.bfloat16), whole[:, start : start + size], NT,
            preferred_element_type=jnp.float32,
        )


def shards(image_emb, image_ids, text_feats, text_ids, text_head):
    bf, f32 = jnp.bfloat16, jnp.float32
    vmem = pl.BlockSpec(memory_space=pltpu.VMEM)
    hbm = pl.BlockSpec(memory_space=pl.ANY)
    dma = pltpu.SemaphoreType.DMA
    scratch = [
        pltpu.VMEM((B, D), bf),
        pltpu.VMEM((B, D), bf),
        pltpu.VMEM((D, D), bf),
        pltpu.VMEM((4, 2, B, D), bf),
        pltpu.VMEM((4, 2, B, D), bf),
        pltpu.VMEM((2 * B, D), bf),
        pltpu.VMEM((2 * B, D), bf),
        pltpu.VMEM((8, 16, B), jnp.int32),
        pltpu.VMEM((2 * B, B), f32),
        pltpu.VMEM((2 * B, B), f32),
        pltpu.VMEM((2 * B, D), f32),
        pltpu.VMEM((2 * B, D), f32),
        pltpu.VMEM((B, D), f32),
        pltpu.VMEM((B, D), f32),
        pltpu.VMEM((B, D), f32),
        pltpu.VMEM((D, B), bf),
        pltpu.VMEM((4, 2, 2, B, D), bf),
        pltpu.VMEM((SLICE, 16 * B), bf),
        pltpu.VMEM((9, SLICE, B), f32),
        pltpu.VMEM((16, SLICE, B), f32),
        pltpu.VMEM((SLICE, B), bf),
        dma((3,)),
    ]
    for n in (48, 7, 4, 16, 16):
        scratch += [dma((n,)), dma((n,))]
    scratch += [dma((9,)), dma((16,)), dma((8,)), dma((9,))]
    for n in (8, 8, 8):
        scratch += [dma((n,)), dma((n,))]
    scratch += [pltpu.VMEM((4, 2, 2, SLICE, D), bf), dma((8,))]
    gimg, gtxt, g = pl.pallas_call(
        kernel,
        out_shape=(
            jax.ShapeDtypeStruct((B, D), bf),
            jax.ShapeDtypeStruct((B, D), bf),
            jax.ShapeDtypeStruct((4, 2, 2, SLICE, D), bf),
        ),
        in_specs=[hbm, vmem, hbm, vmem, hbm],
        out_specs=(vmem, vmem, hbm),
        scratch_shapes=scratch,
        compiler_params=pltpu.CompilerParams(
            collective_id=0, has_side_effects=True, vmem_limit_bytes=60 * 2**20
        ),
    )(image_emb, image_ids.reshape(1, B), text_feats, text_ids.reshape(1, B), text_head)
    fixed = pl.BlockSpec((B, D), lambda n: (0, 0))
    return pl.pallas_call(
        finish,
        grid=(D // WIDE,),
        out_shape=(
            jax.ShapeDtypeStruct((B, D), bf),
            jax.ShapeDtypeStruct((B, D), bf),
            jax.ShapeDtypeStruct((D, D), f32),
        ),
        in_specs=[pl.BlockSpec((4, 2, 2, SLICE, WIDE), lambda n: (0, 0, 0, 0, n)), fixed, fixed],
        out_specs=(fixed, fixed, pl.BlockSpec((WIDE, D), lambda n: (n, 0))),
        scratch_shapes=[pltpu.VMEM((D, WIDE), bf)],
        compiler_params=pltpu.CompilerParams(vmem_limit_bytes=60 * 2**20),
    )(g, gimg, gtxt)


def solution(mesh):
    placed = (P("blk", None), P("blk"), P("blk", None), P("blk"), P())
    return jax.shard_map(
        shards,
        mesh=mesh,
        in_specs=placed,
        out_specs=(P("blk", None), P("blk", None), P()),
        check_vma=False,
    )
```

```python
import jax
import jax.numpy as jnp
from jax import lax
from jax.experimental import pallas as pl
from jax.experimental.pallas import tpu as pltpu
from jax.sharding import PartitionSpec as P

MESH = pl.DeviceIdType.MESH
D = 1152
B = 128
REACH = 6
SLICE = 80
OWNER = (0, 4, 8, 12, 2, 3, 7, 11, 15)
X_LANES = ((256, 384), (640, 256))
X_ALL = (256, 640)
WIDE = 384
NT = (((1,), (1,)), ((), ()))


def start_row(a):
    return pl.multiple_of(16 * ((9 * a) // 2), 16)


def kernel(
    img_hbm, imgid_ref, txt_hbm, txtid_ref, head_hbm,
    gimg_ref, gtxt_ref, g_ref,
    img_ref, txt_ref, head_ref, imgs, txts, img_pair, txt_pair, ids, img_col, txt_col,
    acc_t, acc_i, got_t, got_i, pre, gp_t, feats, gp_in, part, sums, block,
    load, band_s, band_r, id_s, id_r, pair_s, pair_r, f_s, f_r, gp_s, gp_r, rs_s, rs_r,
    az_s, az_r, a2_s, a2_r, a3_s, a3_r, am_s, am_r, g_vm, keep,
):
    loads = [
        pltpu.make_async_copy(a, b, load.at[n])
        for n, (a, b) in enumerate(
            ((img_hbm, img_ref), (txt_hbm, txt_ref), (head_hbm, head_ref))
        )
    ]
    for c in loads:
        c.start()

    me = lax.axis_index("blk")
    core = lax.rem(me, 2)
    z = lax.rem(me // 2, 8)
    x = lax.rem(me // 16, 4)
    y = me // 64
    g, xp = x // 2, lax.rem(x, 2)
    a = (y * 2 + xp) * 2 + core
    b = z * 2 + g

    def at(y2, x2, z2, c2):
        return ((y2 * 4 + x2) * 8 + z2) * 2 + c2

    def of_group(a2):
        return at(a2 // 4, 2 * g + lax.rem(a2 // 2, 2), z, lax.rem(a2, 2))

    def of_column(b2):
        return at(y, 2 * lax.rem(b2, 2) + xp, b2 // 2, core)

    mate = at(y, x, z, 1 - core)
    partner = at(y, x + 1 - 2 * xp, z, core)
    right, left = lax.rem(me + 2, 256), lax.rem(me + 254, 256)
    yp, ym, yo = lax.rem(y + 1, 4), lax.rem(y + 3, 4), lax.rem(y + 2, 4)
    up, down = at(yp, x, z, core), at(ym, x, z, core)

    barrier = pltpu.get_barrier_semaphore()

    def greet(device):
        pl.semaphore_signal(barrier, inc=1, device_id=(device,), device_id_type=MESH)

    for step in (2, 4, 6, 250, 252, 254):
        greet(lax.rem(me + step, 256))
    greet(at(y, 3 - x, z, core))

    def greet_groups(i, carry):
        greet(of_group(lax.rem(a + i, 16)))
        greet(of_column(lax.rem(b + i, 16)))
        return carry

    lax.fori_loop(1, 16, greet_groups, 0)

    sent = []

    def copy(src, dst, ssem, rsem, device):
        return pltpu.make_async_remote_copy(
            src_ref=src, dst_ref=dst, send_sem=ssem, recv_sem=rsem,
            device_id=(device,), device_id_type=MESH,
        )

    def send(src, dst, ssem, rsem, device):
        c = copy(src, dst, ssem, rsem, device)
        c.start()
        sent.append(c)
        return c

    loads[0].wait()
    image_f = img_ref[...].astype(jnp.float32)
    image_inv = lax.rsqrt(jnp.sum(image_f * image_f, axis=-1, keepdims=True) + 1e-06)
    own_z = (image_f * image_inv).astype(jnp.bfloat16)
    imgs[0, 0] = own_z
    img_pair[0:B] = own_z
    ids[0] = jnp.concatenate(
        [
            jnp.broadcast_to(imgid_ref[...], (8, B)),
            jnp.broadcast_to(txtid_ref[...], (8, B)),
        ],
        axis=0,
    )
    loads[1].wait()
    feats[y, xp, core] = txt_ref[...]

    pl.semaphore_wait(barrier, 37)

    hold = {}
    PARTS = (4, 2)

    def idle(kind, step, way):
        return step == 3 and way == kind

    def wanted(kind):
        return core == 1 if kind == 0 else core == 0

    def band_copy(kind, buf, step, way, n):
        rows = pl.ds(n * (B // PARTS[kind]), B // PARTS[kind])
        src = buf.at[0, 0, rows] if step == 1 else buf.at[step - 1, way, rows]
        k = ((kind * 2 + way) * 3 + step - 1) * 4 + n
        return copy(src, buf.at[step, way, rows], band_s.at[k], band_r.at[k], (right, left)[way])

    def band_send(kind, buf, step, way, n):
        if idle(kind, step, way):
            @pl.when(wanted(kind))
            def _():
                band_copy(kind, buf, step, way, n).start()
            return
        c = band_copy(kind, buf, step, way, n)
        c.start()
        sent.append(c)
        hold[kind, step, way, n] = c

    def band_start(kind, buf, first, last):
        for n in range(first, last):
            for way in range(2):
                band_send(kind, buf, 1, way, n)

    def band_pace(n):
        for way in range(2):
            c = hold[0, 1, way, n]
            c.wait_send()
            sent.remove(c)
            band_send(0, imgs, 1, way, n + 2)

    def band_forward(kind, buf, step):
        for n in range(PARTS[kind]):
            for way in range(2):
                hold[kind, step, way, n].wait_recv()
                band_send(kind, buf, step + 1, way, n)

    def band_wait(kind, buf, step):
        for n in range(PARTS[kind]):
            for way in range(2):
                if idle(kind, step, way):
                    @pl.when(wanted(kind))
                    def _():
                        band_copy(kind, buf, step, way, n).wait_recv()
                else:
                    hold[kind, step, way, n].wait_recv()

    band_start(0, imgs, 0, 2)
    id_copies = [send(ids.at[0], ids.at[7], id_s.at[6], id_r.at[6], mate)]
    for n, step in enumerate((2, 4, 6)):
        for way in range(2):
            k = 2 * n + way
            to = lax.rem(me + (step if way == 0 else 256 - step), 256)
            id_copies.append(send(ids.at[0], ids.at[1 + k], id_s.at[k], id_r.at[k], to))

    F = {}

    def feat_copy(k, y2, xp2, device, rows=pl.ds(0, B), arrival=None):
        view = feats.at[y2, xp2, core, rows]
        return copy(view, view, f_s.at[k], f_r.at[k if arrival is None else arrival], device)

    def feat_send(name, *place):
        F[name] = feat_copy(*place)
        F[name].start()
        sent.append(F[name])

    maybe = []

    def feat_when(cond, name, *place):
        c = F[name] = feat_copy(*place)

        @pl.when(cond)
        def _():
            c.start()

        maybe.append((cond, c))

    up_shut, up_help = (x == 0) & (z == 0), (x == 1) & (z == 0)
    down_shut, down_help = (x == 3) & (z == 7), (x == 2) & (z == 7)
    up_open, down_open = jnp.logical_not(up_shut), jnp.logical_not(down_shut)
    other = 1 - xp
    feat_send("x", 0, y, xp, partner)
    feat_when(up_open, "u", 1, y, xp, up)
    feat_when(down_open, "d", 2, y, xp, down)
    img_mate = send(imgs.at[0, 0], img_pair.at[pl.ds(B, B)], pair_s.at[0], pair_r.at[0], mate)
    feat_send("m0", 8 + 0, y, xp, mate)

    low, high = pl.ds(0, B // 2), pl.ds(B // 2, B // 2)

    def feats_second():
        F["x"].wait_recv()
        feat_when(up_open, "xu", 3, y, other, up)
        feat_when(down_open, "xd", 4, y, other, down)
        feat_send("m1", 8 + 1, y, other, mate)

    def feats_up():
        F["u"].wait_recv()
        F["xu"].wait_recv()
        F["m2"].start()
        F["m4"].start()

    def feats_down():
        F["d"].wait_recv()
        F["xd"].wait_recv()
        F["m3"].start()
        F["m5"].start()

    def feats_third():
        for k, y2, xp2 in ((2, ym, xp), (3, yp, xp), (4, ym, other), (5, yp, other)):
            F["m%d" % k] = feat_copy(8 + k, y2, xp2, mate)
            sent.append(F["m%d" % k])
        pl.when(up_open)(feats_up)
        pl.when(down_open)(feats_down)
        low_from, low_to = jnp.where(up_shut, yp, ym), jnp.where(up_shut, down, up)
        high_from, high_to = jnp.where(down_shut, ym, yp), jnp.where(down_shut, up, down)
        feat_send("o0", 5, low_from, xp, low_to, low)
        feat_send("o1", 6, high_from, xp, high_to, high)
        feat_send("xo0", 7, low_from, other, low_to, low)
        feat_send("xo1", 16, high_from, other, high_to, high)
        feat_when(up_help, "hu0", 17, ym, xp, partner, pl.ds(0, B), 3)
        feat_when(up_help, "hu1", 18, ym, other, partner, pl.ds(0, B), 1)
        feat_when(down_help, "hd0", 19, yp, xp, partner, pl.ds(0, B), 4)
        feat_when(down_help, "hd1", 20, yp, other, partner, pl.ds(0, B), 2)

    def feats_fourth():
        F["o0"].wait_recv()
        F["o1"].wait_recv()
        feat_send("m6", 8 + 6, yo, xp, mate)
        F["xo0"].wait_recv()
        F["xo1"].wait_recv()
        feat_send("m7", 8 + 7, yo, other, mate)
        pl.when(up_shut)(feats_up)
        pl.when(down_shut)(feats_down)

    def feats_wait():
        for n in range(8):
            F["m%d" % n].wait_recv()

    @pl.when(core == 0)
    def _():
        imgs[3, 0] = jnp.zeros((B, D), jnp.bfloat16)

    @pl.when(core == 1)
    def _():
        txts[3, 1] = jnp.zeros((B, D), jnp.bfloat16)

    loads[2].wait()
    pre[...] = jnp.dot(txt_ref[...], head_ref[...], preferred_element_type=jnp.float32)
    text_pre = pre[...]
    text_inv = lax.rsqrt(jnp.sum(text_pre * text_pre, axis=-1, keepdims=True) + 1e-06)
    text_z = (text_pre * text_inv).astype(jnp.bfloat16)
    txts[0, 0] = text_z
    txt_pair[0:B] = text_z
    txt_mate = send(txts.at[0, 0], txt_pair.at[pl.ds(B, B)], pair_s.at[1], pair_r.at[1], mate)

    for c in id_copies:
        c.wait_recv()

    def column(row):
        return jnp.transpose(jnp.broadcast_to(row.astype(jnp.float32), (B, B)))

    for h, slot in ((0, 0), (1, 7)):
        img_col[pl.ds(h * B, B)] = column(ids[slot, 0:1])
        txt_col[pl.ds(h * B, B)] = column(ids[slot, 8:9])

    def process(kind, step, here_ref, col_ref, blocks, acc_ref):
        slots = (0,) if step == 0 else (2 * step - 1, 2 * step)
        logit = (
            10.0 * lax.dot_general(here_ref[...], blocks, NT, preferred_element_type=jnp.float32)
            - 5.0
        )
        coefs = []
        for n, slot in enumerate(slots):
            row = ids[slot, 8 * kind : 8 * kind + 1].astype(jnp.float32)
            label = jnp.where(col_ref[...] == row, 1.0, -1.0)
            part_logit = logit[:, n * B : (n + 1) * B]
            coef = -label * jax.nn.sigmoid(-label * part_logit)
            if step == 3:
                delta = 2 * step * (2 * n - 1)
                offset = (delta, delta + 2 * core - 1) if kind == 0 else (-delta, 1 - 2 * core - delta)
                keep = [
                    jnp.where((o >= 1 - REACH) & (o <= REACH), 1.0, 0.0).astype(jnp.float32)
                    for o in offset
                ]
                half = lax.broadcasted_iota(jnp.int32, coef.shape, 0) < B
                coef = coef * jnp.where(half, keep[0], keep[1])
            coefs.append(coef.astype(jnp.bfloat16))
        coef = coefs[0] if len(coefs) == 1 else jnp.concatenate(coefs, axis=1)
        term = jnp.dot(coef, blocks, preferred_element_type=jnp.float32)
        if step == 0:
            acc_ref[...] = term
        else:
            acc_ref[...] += term

    def pair_block(buf, step):
        return buf[step].reshape(2 * B, D)

    def process_images(step):
        process(0, step, txt_pair, txt_col, pair_block(imgs, step), acc_t)

    def process_texts(step):
        process(1, step, img_pair, img_col, pair_block(txts, step), acc_i)

    band_pace(0)
    txt_mate.wait_recv()
    process(0, 0, txt_pair, txt_col, imgs[0, 0], acc_t)
    band_pace(1)
    img_mate.wait_recv()
    process(1, 0, img_pair, img_col, txts[0, 0], acc_i)
    band_forward(0, imgs, 1)
    feats_second()
    process_images(1)
    band_forward(0, imgs, 2)
    feats_third()
    process_images(2)
    band_wait(0, imgs, 3)
    band_start(1, txts, 0, 2)
    process_images(3)
    swap = send(acc_t.at[pl.ds(B, B)], got_t, pair_s.at[2], pair_r.at[2], mate)
    text_unit = pre[...] * text_inv
    swap.wait_recv()
    grad_tz = 10.0 * (acc_t[0:B] + got_t[...])
    grad_pre = (
        grad_tz - text_unit * jnp.sum(text_unit * grad_tz, axis=-1, keepdims=True)
    ) * text_inv
    for n in range(9):
        gp_t[n * B : (n + 1) * B] = jnp.transpose(grad_pre[:, n * B : (n + 1) * B]).astype(
            jnp.bfloat16
        )
    grad_pre = grad_pre.astype(jnp.bfloat16)

    def gp_copy(i):
        a2 = lax.rem(a + i, 16)
        return copy(
            gp_t.at[pl.ds(start_row(a2), SLICE)],
            gp_in.at[:, pl.ds(pl.multiple_of(a * B, B), B)],
            gp_s.at[i], gp_r.at[i], of_group(a2),
        )

    def gp_send(i, carry):
        gp_copy(i).start()
        return carry

    lax.fori_loop(1, 16, gp_send, 0)
    gp_in[:, pl.ds(pl.multiple_of(a * B, B), B)] = gp_t[pl.ds(start_row(a), SLICE)]
    feats_fourth()
    gtxt_ref[...] = lax.dot_general(
        grad_pre, head_ref[...], NT, preferred_element_type=jnp.float32
    ).astype(jnp.bfloat16)
    band_forward(1, txts, 1)
    feats_wait()

    def gp_wait(i, carry):
        gp_copy(i).wait_recv()
        return carry

    lax.fori_loop(1, 16, gp_wait, 0)
    slices = jnp.dot(gp_in[...], feats[...].reshape(16 * B, D), preferred_element_type=jnp.float32)
    for n in range(9):
        part[n] = slices[:, n * B : (n + 1) * B].astype(jnp.bfloat16)

    def rs_copy(n, to):
        return copy(part.at[n], sums.at[b], rs_s.at[n], rs_r.at[b], of_column(to))

    for n, to in enumerate(OWNER):
        @pl.when(b != to)
        def _():
            rs_copy(n, to).start()

        @pl.when(b == to)
        def _():
            sums[b] = part[n]

    process_texts(1)
    band_forward(1, txts, 2)
    mine = jnp.where(g == 0, jnp.where(b == 2, 4, z // 2), 5 + z // 2)
    is_owner = jnp.logical_or(lax.rem(z, 2) == g, b == 2)
    lanes = pl.ds(pl.multiple_of(mine * B, B), B)

    def az_copy(i):
        return copy(
            block, g_vm.at[y, xp, core, :, lanes], az_s.at[i], az_r.at[mine],
            at(y, x, lax.rem(z + i, 8), core),
        )

    @pl.when(is_owner)
    def _():
        def rs_wait(i, carry):
            b2 = lax.rem(b + i, 16)
            copy(part.at[0], sums.at[b2], rs_s.at[0], rs_r.at[b2], mate).wait_recv()
            return carry

        lax.fori_loop(1, 16, rs_wait, 0)
        total = sums[0].astype(jnp.float32)
        for n in range(1, 16):
            total = total + sums[n].astype(jnp.float32)
        block[...] = total.astype(jnp.bfloat16)
        g_vm[y, xp, core, :, lanes] = total.astype(jnp.bfloat16)

        def az_send(i, carry):
            az_copy(i).start()
            return carry

        lax.fori_loop(1, 8, az_send, 0)

    for gg, (first, count) in enumerate(((0, 5), (5, 4))):
        for n in range(first, first + count):
            @pl.when((g == gg) & (b != OWNER[n]))
            def _():
                copy(
                    block, g_vm.at[y, xp, core, :, pl.ds(n * B, B)], az_s.at[0], az_r.at[n], mate
                ).wait_recv()

    def lanes_y(g2):
        return pl.ds(pl.multiple_of(896 * g2, B), 256)

    def back(x2, i):
        return lax.rem(x2 + 4 - i, 4)

    def along_x(i):
        return at(y, lax.rem(x + i, 4), z, core)

    def along_y(i):
        return at(lax.rem(y + i, 4), x, z, core)

    def second_x(i, gg):
        view = g_vm.at[y, xp, core, :, pl.ds(*X_LANES[gg])]
        return copy(view, view, a2_s.at[i], a2_r.at[i], along_x(i))

    def second_y(i):
        view = g_vm.at[y, xp, core, :, lanes_y(g)]
        return copy(view, view, a2_s.at[4 + i], a2_r.at[4 + i], along_y(i))

    def third_x(i):
        view = g_vm.at[y, :, core, :, pl.ds(*X_ALL)]
        return copy(view, view, a3_s.at[i], a3_r.at[i], along_y(i))

    def third_y(i):
        view = g_vm.at[:, xp, core, :, lanes_y(g)]
        return copy(view, view, a3_s.at[4 + i], a3_r.at[4 + i], along_x(i))

    def place_x(ref, i, c2):
        return ref.at[back(y, i), :, c2, :, pl.ds(*X_ALL)]

    def place_y(ref, i, c2):
        x2 = back(x, i)
        return ref.at[:, lax.rem(x2, 2), c2, :, lanes_y(x2 // 2)]

    def mate_x(i, c2):
        return copy(place_x(g_vm, i, c2), place_x(g_ref, i, c2), am_s.at[i], am_r.at[i], mate)

    def mate_y(i, c2):
        return copy(
            place_y(g_vm, i, c2), place_y(g_ref, i, c2), am_s.at[4 + i], am_r.at[4 + i], mate
        )

    def keep_x(i):
        return pltpu.make_async_copy(place_x(g_vm, i, core), place_x(g_ref, i, core), keep.at[i])

    def keep_y(i):
        return pltpu.make_async_copy(
            place_y(g_vm, i, core), place_y(g_ref, i, core), keep.at[4 + i]
        )

    ORDER = (1, 3, 2)
    for i in ORDER:
        for gg in range(2):
            @pl.when(g == gg)
            def _():
                second_x(i, gg).start()
        second_y(i).start()
    process_texts(2)
    for i in ORDER:
        for gg in range(2):
            @pl.when(back(x, i) // 2 == gg)
            def _():
                second_x(i, gg).wait_recv()
    for i in ORDER:
        third_x(i).start()
    for i in ORDER:
        second_y(i).wait_recv()
    for i in ORDER:
        third_y(i).start()
    mate_x(0, core).start()
    keep_x(0).start()
    mate_y(0, core).start()
    keep_y(0).start()


    band_wait(1, txts, 3)
    process_texts(3)
    swap_i = send(acc_i.at[pl.ds(B, B)], got_i, pair_s.at[3], pair_r.at[3], mate)
    third_x(1).wait_recv()
    mate_x(1, core).start()
    keep_x(1).start()
    third_y(1).wait_recv()
    mate_y(1, core).start()
    keep_y(1).start()
    third_x(3).wait_recv()
    mate_x(3, core).start()
    keep_x(3).start()
    third_y(3).wait_recv()
    mate_y(3, core).start()
    keep_y(3).start()
    third_x(2).wait_recv()
    mate_x(2, core).start()
    keep_x(2).start()
    third_y(2).wait_recv()
    mate_y(2, core).start()
    keep_y(2).start()
    swap_i.wait_recv()
    grad_iz = 10.0 * (acc_i[0:B] + got_i[...])
    image_g = img_ref[...].astype(jnp.float32)
    image_unit = image_g * image_inv
    gimg_ref[...] = (
        (grad_iz - image_unit * jnp.sum(image_unit * grad_iz, axis=-1, keepdims=True)) * image_inv
    ).astype(jnp.bfloat16)

    for cond, c in maybe:
        pl.when(cond)(c.wait_send)
    for kind, buf in ((0, imgs), (1, txts)):
        @pl.when(wanted(kind))
        def _():
            for n in range(PARTS[kind]):
                band_copy(kind, buf, 3, kind, n).wait_send()
    for c in sent:
        c.wait_send()

    def gp_drain(i, carry):
        gp_copy(i).wait_send()
        return carry

    lax.fori_loop(1, 16, gp_drain, 0)
    for n, to in enumerate(OWNER):
        @pl.when(b != to)
        def _():
            rs_copy(n, to).wait_send()

    @pl.when(is_owner)
    def _():
        def az_drain(i, carry):
            az_copy(i).wait_send()
            return carry

        lax.fori_loop(1, 8, az_drain, 0)

    for i in ORDER:
        for gg in range(2):
            @pl.when(g == gg)
            def _():
                second_x(i, gg).wait_send()
        second_y(i).wait_send()
        third_x(i).wait_send()
        third_y(i).wait_send()
    for i in range(4):
        keep_x(i).wait()
        keep_y(i).wait()
        mate_x(i, core).wait_send()
        mate_y(i, core).wait_send()
        mate_x(i, 1 - core).wait_recv()
        mate_y(i, 1 - core).wait_recv()


def finish(g_ref, gimg_ref, gtxt_ref, oimg_ref, otxt_ref, ohead_ref, whole):
    @pl.when(pl.program_id(0) == 0)
    def _():
        oimg_ref[...] = gimg_ref[...]
        otxt_ref[...] = gtxt_ref[...]

    for a in range(16):
        view = g_ref[a // 4, (a // 2) % 2, a % 2]
        if a % 2 == 0:
            whole[72 * a : 72 * a + 80] = view
        else:
            whole[72 * a + 8 : 72 * a + 72] = view[16:80]
    for start, size in ((0, 256), (256, 128)):
        eye = lax.broadcasted_iota(jnp.int32, (size, size), 0) == lax.broadcasted_iota(
            jnp.int32, (size, size), 1
        )
        ohead_ref[start : start + size] = lax.dot_general(
            eye.astype(jnp.bfloat16), whole[:, start : start + size], NT,
            preferred_element_type=jnp.float32,
        )


def shards(image_emb, image_ids, text_feats, text_ids, text_head):
    bf, f32 = jnp.bfloat16, jnp.float32
    vmem = pl.BlockSpec(memory_space=pltpu.VMEM)
    hbm = pl.BlockSpec(memory_space=pl.ANY)
    dma = pltpu.SemaphoreType.DMA
    scratch = [
        pltpu.VMEM((B, D), bf),
        pltpu.VMEM((B, D), bf),
        pltpu.VMEM((D, D), bf),
        pltpu.VMEM((4, 2, B, D), bf),
        pltpu.VMEM((4, 2, B, D), bf),
        pltpu.VMEM((2 * B, D), bf),
        pltpu.VMEM((2 * B, D), bf),
        pltpu.VMEM((8, 16, B), jnp.int32),
        pltpu.VMEM((2 * B, B), f32),
        pltpu.VMEM((2 * B, B), f32),
        pltpu.VMEM((2 * B, D), f32),
        pltpu.VMEM((2 * B, D), f32),
        pltpu.VMEM((B, D), f32),
        pltpu.VMEM((B, D), f32),
        pltpu.VMEM((B, D), f32),
        pltpu.VMEM((D, B), bf),
        pltpu.VMEM((4, 2, 2, B, D), bf),
        pltpu.VMEM((SLICE, 16 * B), bf),
        pltpu.VMEM((9, SLICE, B), bf),
        pltpu.VMEM((16, SLICE, B), bf),
        pltpu.VMEM((SLICE, B), bf),
        dma((3,)),
    ]
    for n in (48, 7, 4, 21, 16):
        scratch += [dma((n,)), dma((n,))]
    scratch += [dma((9,)), dma((16,)), dma((8,)), dma((9,))]
    for n in (8, 8, 8):
        scratch += [dma((n,)), dma((n,))]
    scratch += [pltpu.VMEM((4, 2, 2, SLICE, D), bf), dma((8,))]
    gimg, gtxt, g = pl.pallas_call(
        kernel,
        out_shape=(
            jax.ShapeDtypeStruct((B, D), bf),
            jax.ShapeDtypeStruct((B, D), bf),
            jax.ShapeDtypeStruct((4, 2, 2, SLICE, D), bf),
        ),
        in_specs=[hbm, vmem, hbm, vmem, hbm],
        out_specs=(vmem, vmem, hbm),
        scratch_shapes=scratch,
        compiler_params=pltpu.CompilerParams(
            collective_id=0, has_side_effects=True, vmem_limit_bytes=60 * 2**20
        ),
    )(image_emb, image_ids.reshape(1, B), text_feats, text_ids.reshape(1, B), text_head)
    fixed = pl.BlockSpec((B, D), lambda n: (0, 0))
    return pl.pallas_call(
        finish,
        grid=(D // WIDE,),
        out_shape=(
            jax.ShapeDtypeStruct((B, D), bf),
            jax.ShapeDtypeStruct((B, D), bf),
            jax.ShapeDtypeStruct((D, D), f32),
        ),
        in_specs=[pl.BlockSpec((4, 2, 2, SLICE, WIDE), lambda n: (0, 0, 0, 0, n)), fixed, fixed],
        out_specs=(fixed, fixed, pl.BlockSpec((WIDE, D), lambda n: (n, 0))),
        scratch_shapes=[pltpu.VMEM((D, WIDE), bf)],
        compiler_params=pltpu.CompilerParams(vmem_limit_bytes=60 * 2**20),
    )(g, gimg, gtxt)


def solution(mesh):
    placed = (P("blk", None), P("blk"), P("blk", None), P("blk"), P())
    return jax.shard_map(
        shards,
        mesh=mesh,
        in_specs=placed,
        out_specs=(P("blk", None), P("blk", None), P()),
        check_vma=False,
    )
```

```python
import jax
import jax.numpy as jnp
from jax import lax
from jax.experimental import pallas as pl
from jax.experimental.pallas import tpu as pltpu
from jax.sharding import PartitionSpec as P

MESH = pl.DeviceIdType.MESH
D = 1152
B = 128
REACH = 6
SLICE = 80
OWNER = (0, 4, 8, 12, 2, 3, 7, 11, 15)
X_LANES = ((256, 384), (640, 256))
X_ALL = (256, 640)
WIDE = 384
NT = (((1,), (1,)), ((), ()))


def start_row(a):
    return pl.multiple_of(16 * ((9 * a) // 2), 16)


def kernel(
    img_hbm, imgid_ref, txt_hbm, txtid_ref, head_hbm,
    gimg_ref, gtxt_ref, g_ref,
    img_ref, txt_ref, head_ref, imgs, txts, img_pair, txt_pair, ids, img_col, txt_col,
    acc_t, acc_i, got_t, got_i, pre, gp_t, feats, gp_in, part, sums, block,
    load, band_s, band_r, id_s, id_r, pair_s, pair_r, f_s, f_r, gp_s, gp_r, rs_s, rs_r,
    az_s, az_r, a2_s, a2_r, a3_s, a3_r, am_s, am_r, g_vm, keep,
):
    loads = [
        pltpu.make_async_copy(a, b, load.at[n])
        for n, (a, b) in enumerate(
            ((img_hbm, img_ref), (txt_hbm, txt_ref), (head_hbm, head_ref))
        )
    ]
    for c in loads:
        c.start()

    me = lax.axis_index("blk")
    core = lax.rem(me, 2)
    z = lax.rem(me // 2, 8)
    x = lax.rem(me // 16, 4)
    y = me // 64
    g, xp = x // 2, lax.rem(x, 2)
    a = (y * 2 + xp) * 2 + core
    b = z * 2 + g

    def at(y2, x2, z2, c2):
        return ((y2 * 4 + x2) * 8 + z2) * 2 + c2

    def of_group(a2):
        return at(a2 // 4, 2 * g + lax.rem(a2 // 2, 2), z, lax.rem(a2, 2))

    def of_column(b2):
        return at(y, 2 * lax.rem(b2, 2) + xp, b2 // 2, core)

    mate = at(y, x, z, 1 - core)
    partner = at(y, x + 1 - 2 * xp, z, core)
    right, left = lax.rem(me + 2, 256), lax.rem(me + 254, 256)
    yp, ym, yo = lax.rem(y + 1, 4), lax.rem(y + 3, 4), lax.rem(y + 2, 4)
    up, down = at(yp, x, z, core), at(ym, x, z, core)

    barrier = pltpu.get_barrier_semaphore()

    def greet(device):
        pl.semaphore_signal(barrier, inc=1, device_id=(device,), device_id_type=MESH)

    for step in (2, 4, 6, 250, 252, 254):
        greet(lax.rem(me + step, 256))
    greet(at(y, 3 - x, z, core))

    def greet_groups(i, carry):
        greet(of_group(lax.rem(a + i, 16)))
        greet(of_column(lax.rem(b + i, 16)))
        return carry

    lax.fori_loop(1, 16, greet_groups, 0)

    sent = []

    def copy(src, dst, ssem, rsem, device):
        return pltpu.make_async_remote_copy(
            src_ref=src, dst_ref=dst, send_sem=ssem, recv_sem=rsem,
            device_id=(device,), device_id_type=MESH,
        )

    def send(src, dst, ssem, rsem, device):
        c = copy(src, dst, ssem, rsem, device)
        c.start()
        sent.append(c)
        return c

    loads[0].wait()
    image_f = img_ref[...].astype(jnp.float32)
    image_inv = lax.rsqrt(jnp.sum(image_f * image_f, axis=-1, keepdims=True) + 1e-06)
    own_z = (image_f * image_inv).astype(jnp.bfloat16)
    imgs[0, 0] = own_z
    img_pair[0:B] = own_z
    ids[0] = jnp.concatenate(
        [
            jnp.broadcast_to(imgid_ref[...], (8, B)),
            jnp.broadcast_to(txtid_ref[...], (8, B)),
        ],
        axis=0,
    )
    loads[1].wait()
    feats[y, xp, core] = txt_ref[...]

    pl.semaphore_wait(barrier, 37)

    hold = {}
    PARTS = (4, 2)

    def idle(kind, step, way):
        return step == 3 and way == kind

    def wanted(kind):
        return core == 1 if kind == 0 else core == 0

    def band_copy(kind, buf, step, way, n):
        rows = pl.ds(n * (B // PARTS[kind]), B // PARTS[kind])
        src = buf.at[0, 0, rows] if step == 1 else buf.at[step - 1, way, rows]
        k = ((kind * 2 + way) * 3 + step - 1) * 4 + n
        return copy(src, buf.at[step, way, rows], band_s.at[k], band_r.at[k], (right, left)[way])

    def band_send(kind, buf, step, way, n):
        if idle(kind, step, way):
            @pl.when(wanted(kind))
            def _():
                band_copy(kind, buf, step, way, n).start()
            return
        c = band_copy(kind, buf, step, way, n)
        c.start()
        sent.append(c)
        hold[kind, step, way, n] = c

    def band_start(kind, buf, first, last):
        for n in range(first, last):
            for way in range(2):
                band_send(kind, buf, 1, way, n)

    def band_pace(n):
        for way in range(2):
            c = hold[0, 1, way, n]
            c.wait_send()
            sent.remove(c)
            band_send(0, imgs, 1, way, n + 2)

    def band_forward(kind, buf, step):
        for n in range(PARTS[kind]):
            for way in range(2):
                hold[kind, step, way, n].wait_recv()
                band_send(kind, buf, step + 1, way, n)

    def band_wait(kind, buf, step):
        for n in range(PARTS[kind]):
            for way in range(2):
                if idle(kind, step, way):
                    @pl.when(wanted(kind))
                    def _():
                        band_copy(kind, buf, step, way, n).wait_recv()
                else:
                    hold[kind, step, way, n].wait_recv()

    band_start(0, imgs, 0, 2)
    id_copies = [send(ids.at[0], ids.at[7], id_s.at[6], id_r.at[6], mate)]
    for n, step in enumerate((2, 4, 6)):
        for way in range(2):
            k = 2 * n + way
            to = lax.rem(me + (step if way == 0 else 256 - step), 256)
            id_copies.append(send(ids.at[0], ids.at[1 + k], id_s.at[k], id_r.at[k], to))

    F = {}

    def feat_copy(k, y2, xp2, device, rows=pl.ds(0, B), arrival=None):
        view = feats.at[y2, xp2, core, rows]
        return copy(view, view, f_s.at[k], f_r.at[k if arrival is None else arrival], device)

    def feat_send(name, *place):
        F[name] = feat_copy(*place)
        F[name].start()
        sent.append(F[name])

    maybe = []

    def feat_when(cond, name, *place):
        c = F[name] = feat_copy(*place)

        @pl.when(cond)
        def _():
            c.start()

        maybe.append((cond, c))

    up_shut, up_help = (x == 0) & (z == 0), (x == 1) & (z == 0)
    down_shut, down_help = (x == 3) & (z == 7), (x == 2) & (z == 7)
    up_open, down_open = jnp.logical_not(up_shut), jnp.logical_not(down_shut)
    other = 1 - xp
    feat_send("x", 0, y, xp, partner)
    feat_when(up_open, "u", 1, y, xp, up)
    feat_when(down_open, "d", 2, y, xp, down)
    img_mate = send(imgs.at[0, 0], img_pair.at[pl.ds(B, B)], pair_s.at[0], pair_r.at[0], mate)
    feat_send("m0", 8 + 0, y, xp, mate)

    low, high = pl.ds(0, B // 2), pl.ds(B // 2, B // 2)

    def feats_second():
        F["x"].wait_recv()
        feat_when(up_open, "xu", 3, y, other, up)
        feat_when(down_open, "xd", 4, y, other, down)
        feat_send("m1", 8 + 1, y, other, mate)

    def feats_up():
        F["u"].wait_recv()
        F["xu"].wait_recv()
        F["m2"].start()
        F["m4"].start()

    def feats_down():
        F["d"].wait_recv()
        F["xd"].wait_recv()
        F["m3"].start()
        F["m5"].start()

    def feats_third():
        for k, y2, xp2 in ((2, ym, xp), (3, yp, xp), (4, ym, other), (5, yp, other)):
            F["m%d" % k] = feat_copy(8 + k, y2, xp2, mate)
            sent.append(F["m%d" % k])
        pl.when(up_open)(feats_up)
        pl.when(down_open)(feats_down)
        low_from, low_to = jnp.where(up_shut, yp, ym), jnp.where(up_shut, down, up)
        high_from, high_to = jnp.where(down_shut, ym, yp), jnp.where(down_shut, up, down)
        feat_send("o0", 5, low_from, xp, low_to, low)
        feat_send("o1", 6, high_from, xp, high_to, high)
        feat_send("xo0", 7, low_from, other, low_to, low)
        feat_send("xo1", 16, high_from, other, high_to, high)
        feat_when(up_help, "hu0", 17, ym, xp, partner, pl.ds(0, B), 3)
        feat_when(up_help, "hu1", 18, ym, other, partner, pl.ds(0, B), 1)
        feat_when(down_help, "hd0", 19, yp, xp, partner, pl.ds(0, B), 4)
        feat_when(down_help, "hd1", 20, yp, other, partner, pl.ds(0, B), 2)

    def feats_fourth():
        F["o0"].wait_recv()
        F["o1"].wait_recv()
        feat_send("m6", 8 + 6, yo, xp, mate)
        F["xo0"].wait_recv()
        F["xo1"].wait_recv()
        feat_send("m7", 8 + 7, yo, other, mate)
        pl.when(up_shut)(feats_up)
        pl.when(down_shut)(feats_down)

    def feats_wait():
        for n in range(8):
            F["m%d" % n].wait_recv()

    @pl.when(core == 0)
    def _():
        imgs[3, 0] = jnp.zeros((B, D), jnp.bfloat16)

    @pl.when(core == 1)
    def _():
        txts[3, 1] = jnp.zeros((B, D), jnp.bfloat16)

    loads[2].wait()
    pre[...] = jnp.dot(txt_ref[...], head_ref[...], preferred_element_type=jnp.float32)
    text_pre = pre[...]
    text_inv = lax.rsqrt(jnp.sum(text_pre * text_pre, axis=-1, keepdims=True) + 1e-06)
    text_z = (text_pre * text_inv).astype(jnp.bfloat16)
    txts[0, 0] = text_z
    txt_pair[0:B] = text_z
    txt_mate = send(txts.at[0, 0], txt_pair.at[pl.ds(B, B)], pair_s.at[1], pair_r.at[1], mate)

    for c in id_copies:
        c.wait_recv()

    def column(row):
        return jnp.transpose(jnp.broadcast_to(row.astype(jnp.float32), (B, B)))

    for h, slot in ((0, 0), (1, 7)):
        img_col[pl.ds(h * B, B)] = column(ids[slot, 0:1])
        txt_col[pl.ds(h * B, B)] = column(ids[slot, 8:9])

    def process(kind, step, here_ref, col_ref, blocks, acc_ref):
        slots = (0,) if step == 0 else (2 * step - 1, 2 * step)
        logit = (
            10.0 * lax.dot_general(here_ref[...], blocks, NT, preferred_element_type=jnp.float32)
            - 5.0
        )
        coefs = []
        for n, slot in enumerate(slots):
            row = ids[slot, 8 * kind : 8 * kind + 1].astype(jnp.float32)
            label = jnp.where(col_ref[...] == row, 1.0, -1.0)
            part_logit = logit[:, n * B : (n + 1) * B]
            coef = -label * jax.nn.sigmoid(-label * part_logit)
            if step == 3:
                delta = 2 * step * (2 * n - 1)
                offset = (delta, delta + 2 * core - 1) if kind == 0 else (-delta, 1 - 2 * core - delta)
                keep = [
                    jnp.where((o >= 1 - REACH) & (o <= REACH), 1.0, 0.0).astype(jnp.float32)
                    for o in offset
                ]
                half = lax.broadcasted_iota(jnp.int32, coef.shape, 0) < B
                coef = coef * jnp.where(half, keep[0], keep[1])
            coefs.append(coef.astype(jnp.bfloat16))
        coef = coefs[0] if len(coefs) == 1 else jnp.concatenate(coefs, axis=1)
        term = jnp.dot(coef, blocks, preferred_element_type=jnp.float32)
        if step == 0:
            acc_ref[...] = term
        else:
            acc_ref[...] += term

    def pair_block(buf, step):
        return buf[step].reshape(2 * B, D)

    def process_images(step):
        process(0, step, txt_pair, txt_col, pair_block(imgs, step), acc_t)

    def process_texts(step):
        process(1, step, img_pair, img_col, pair_block(txts, step), acc_i)

    band_pace(0)
    txt_mate.wait_recv()
    process(0, 0, txt_pair, txt_col, imgs[0, 0], acc_t)
    band_pace(1)
    img_mate.wait_recv()
    process(1, 0, img_pair, img_col, txts[0, 0], acc_i)
    band_forward(0, imgs, 1)
    feats_second()
    process_images(1)
    band_forward(0, imgs, 2)
    feats_third()
    process_images(2)
    band_wait(0, imgs, 3)
    band_start(1, txts, 0, 2)
    process_images(3)
    swap = send(acc_t.at[pl.ds(B, B)], got_t, pair_s.at[2], pair_r.at[2], mate)
    text_unit = pre[...] * text_inv
    swap.wait_recv()
    grad_tz = 10.0 * (acc_t[0:B] + got_t[...])
    grad_pre = (
        grad_tz - text_unit * jnp.sum(text_unit * grad_tz, axis=-1, keepdims=True)
    ) * text_inv
    for n in range(9):
        gp_t[n * B : (n + 1) * B] = jnp.transpose(grad_pre[:, n * B : (n + 1) * B]).astype(
            jnp.bfloat16
        )
    grad_pre = grad_pre.astype(jnp.bfloat16)

    def gp_copy(i):
        a2 = lax.rem(a + i, 16)
        return copy(
            gp_t.at[pl.ds(start_row(a2), SLICE)],
            gp_in.at[:, pl.ds(pl.multiple_of(a * B, B), B)],
            gp_s.at[i], gp_r.at[i], of_group(a2),
        )

    def gp_send(i, carry):
        gp_copy(i).start()
        return carry

    lax.fori_loop(1, 16, gp_send, 0)
    gp_in[:, pl.ds(pl.multiple_of(a * B, B), B)] = gp_t[pl.ds(start_row(a), SLICE)]
    band_forward(1, txts, 1)
    feats_fourth()
    gtxt_ref[...] = lax.dot_general(
        grad_pre, head_ref[...], NT, preferred_element_type=jnp.float32
    ).astype(jnp.bfloat16)
    feats_wait()

    def gp_wait(i, carry):
        gp_copy(i).wait_recv()
        return carry

    lax.fori_loop(1, 16, gp_wait, 0)
    def rs_copy(n, to):
        return copy(part.at[n], sums.at[b], rs_s.at[n], rs_r.at[b], of_column(to))

    for first in range(0, 9, 2):
        blocks = range(first, min(first + 2, 9))
        columns = feats[:, :, :, :, first * B : blocks.stop * B].reshape(16 * B, len(blocks) * B)
        slices = jnp.dot(gp_in[...], columns, preferred_element_type=jnp.float32)
        for n in blocks:
            part[n] = slices[:, (n - first) * B : (n - first + 1) * B].astype(jnp.bfloat16)

            @pl.when(b != OWNER[n])
            def _():
                rs_copy(n, OWNER[n]).start()

            @pl.when(b == OWNER[n])
            def _():
                sums[b] = part[n]

    process_texts(1)
    band_forward(1, txts, 2)
    mine = jnp.where(g == 0, jnp.where(b == 2, 4, z // 2), 5 + z // 2)
    is_owner = jnp.logical_or(lax.rem(z, 2) == g, b == 2)
    lanes = pl.ds(pl.multiple_of(mine * B, B), B)

    def az_copy(i):
        return copy(
            block, g_vm.at[y, xp, core, :, lanes], az_s.at[i], az_r.at[mine],
            at(y, x, lax.rem(z + i, 8), core),
        )

    @pl.when(is_owner)
    def _():
        def rs_wait(i, carry):
            b2 = lax.rem(b + i, 16)
            copy(part.at[0], sums.at[b2], rs_s.at[0], rs_r.at[b2], mate).wait_recv()
            return carry

        lax.fori_loop(1, 16, rs_wait, 0)
        total = sums[0].astype(jnp.float32)
        for n in range(1, 16):
            total = total + sums[n].astype(jnp.float32)
        block[...] = total.astype(jnp.bfloat16)
        g_vm[y, xp, core, :, lanes] = total.astype(jnp.bfloat16)

        def az_send(i, carry):
            az_copy(i).start()
            return carry

        lax.fori_loop(1, 8, az_send, 0)

    for gg, (first, count) in enumerate(((0, 5), (5, 4))):
        for n in range(first, first + count):
            @pl.when((g == gg) & (b != OWNER[n]))
            def _():
                copy(
                    block, g_vm.at[y, xp, core, :, pl.ds(n * B, B)], az_s.at[0], az_r.at[n], mate
                ).wait_recv()

    def lanes_y(g2):
        return pl.ds(pl.multiple_of(896 * g2, B), 256)

    def back(x2, i):
        return lax.rem(x2 + 4 - i, 4)

    def along_x(i):
        return at(y, lax.rem(x + i, 4), z, core)

    def along_y(i):
        return at(lax.rem(y + i, 4), x, z, core)

    def second_x(i, gg):
        view = g_vm.at[y, xp, core, :, pl.ds(*X_LANES[gg])]
        return copy(view, view, a2_s.at[i], a2_r.at[i], along_x(i))

    def second_y(i):
        view = g_vm.at[y, xp, core, :, lanes_y(g)]
        return copy(view, view, a2_s.at[4 + i], a2_r.at[4 + i], along_y(i))

    def third_x(i):
        view = g_vm.at[y, :, core, :, pl.ds(*X_ALL)]
        return copy(view, view, a3_s.at[i], a3_r.at[i], along_y(i))

    def third_y(i):
        view = g_vm.at[:, xp, core, :, lanes_y(g)]
        return copy(view, view, a3_s.at[4 + i], a3_r.at[4 + i], along_x(i))

    def place_x(ref, i, c2):
        return ref.at[back(y, i), :, c2, :, pl.ds(*X_ALL)]

    def place_y(ref, i, c2):
        x2 = back(x, i)
        return ref.at[:, lax.rem(x2, 2), c2, :, lanes_y(x2 // 2)]

    def mate_x(i, c2):
        return copy(place_x(g_vm, i, c2), place_x(g_ref, i, c2), am_s.at[i], am_r.at[i], mate)

    def mate_y(i, c2):
        return copy(
            place_y(g_vm, i, c2), place_y(g_ref, i, c2), am_s.at[4 + i], am_r.at[4 + i], mate
        )

    def keep_x(i):
        return pltpu.make_async_copy(place_x(g_vm, i, core), place_x(g_ref, i, core), keep.at[i])

    def keep_y(i):
        return pltpu.make_async_copy(
            place_y(g_vm, i, core), place_y(g_ref, i, core), keep.at[4 + i]
        )

    ORDER = (1, 3, 2)
    for i in ORDER:
        for gg in range(2):
            @pl.when(g == gg)
            def _():
                second_x(i, gg).start()
        second_y(i).start()
    process_texts(2)
    for i in ORDER:
        for gg in range(2):
            @pl.when(back(x, i) // 2 == gg)
            def _():
                second_x(i, gg).wait_recv()
    for i in ORDER:
        third_x(i).start()
    for i in ORDER:
        second_y(i).wait_recv()
    for i in ORDER:
        third_y(i).start()
    mate_x(0, core).start()
    keep_x(0).start()
    mate_y(0, core).start()
    keep_y(0).start()


    band_wait(1, txts, 3)
    process_texts(3)
    swap_i = send(acc_i.at[pl.ds(B, B)], got_i, pair_s.at[3], pair_r.at[3], mate)
    third_x(1).wait_recv()
    mate_x(1, core).start()
    keep_x(1).start()
    third_y(1).wait_recv()
    mate_y(1, core).start()
    keep_y(1).start()
    third_x(3).wait_recv()
    mate_x(3, core).start()
    keep_x(3).start()
    third_y(3).wait_recv()
    mate_y(3, core).start()
    keep_y(3).start()
    third_x(2).wait_recv()
    mate_x(2, core).start()
    keep_x(2).start()
    third_y(2).wait_recv()
    mate_y(2, core).start()
    keep_y(2).start()
    swap_i.wait_recv()
    grad_iz = 10.0 * (acc_i[0:B] + got_i[...])
    image_g = img_ref[...].astype(jnp.float32)
    image_unit = image_g * image_inv
    gimg_ref[...] = (
        (grad_iz - image_unit * jnp.sum(image_unit * grad_iz, axis=-1, keepdims=True)) * image_inv
    ).astype(jnp.bfloat16)

    for cond, c in maybe:
        pl.when(cond)(c.wait_send)
    for kind, buf in ((0, imgs), (1, txts)):
        @pl.when(wanted(kind))
        def _():
            for n in range(PARTS[kind]):
                band_copy(kind, buf, 3, kind, n).wait_send()
    for c in sent:
        c.wait_send()

    def gp_drain(i, carry):
        gp_copy(i).wait_send()
        return carry

    lax.fori_loop(1, 16, gp_drain, 0)
    for n, to in enumerate(OWNER):
        @pl.when(b != to)
        def _():
            rs_copy(n, to).wait_send()

    @pl.when(is_owner)
    def _():
        def az_drain(i, carry):
            az_copy(i).wait_send()
            return carry

        lax.fori_loop(1, 8, az_drain, 0)

    for i in ORDER:
        for gg in range(2):
            @pl.when(g == gg)
            def _():
                second_x(i, gg).wait_send()
        second_y(i).wait_send()
        third_x(i).wait_send()
        third_y(i).wait_send()
    for i in range(4):
        keep_x(i).wait()
        keep_y(i).wait()
        mate_x(i, core).wait_send()
        mate_y(i, core).wait_send()
        mate_x(i, 1 - core).wait_recv()
        mate_y(i, 1 - core).wait_recv()


def finish(g_ref, gimg_ref, gtxt_ref, oimg_ref, otxt_ref, ohead_ref, whole):
    @pl.when(pl.program_id(0) == 0)
    def _():
        oimg_ref[...] = gimg_ref[...]
        otxt_ref[...] = gtxt_ref[...]

    for a in range(16):
        view = g_ref[a // 4, (a // 2) % 2, a % 2]
        if a % 2 == 0:
            whole[72 * a : 72 * a + 80] = view
        else:
            whole[72 * a + 8 : 72 * a + 72] = view[16:80]
    for start, size in ((0, 256), (256, 128)):
        eye = lax.broadcasted_iota(jnp.int32, (size, size), 0) == lax.broadcasted_iota(
            jnp.int32, (size, size), 1
        )
        ohead_ref[start : start + size] = lax.dot_general(
            eye.astype(jnp.bfloat16), whole[:, start : start + size], NT,
            preferred_element_type=jnp.float32,
        )


def shards(image_emb, image_ids, text_feats, text_ids, text_head):
    bf, f32 = jnp.bfloat16, jnp.float32
    vmem = pl.BlockSpec(memory_space=pltpu.VMEM)
    hbm = pl.BlockSpec(memory_space=pl.ANY)
    dma = pltpu.SemaphoreType.DMA
    scratch = [
        pltpu.VMEM((B, D), bf),
        pltpu.VMEM((B, D), bf),
        pltpu.VMEM((D, D), bf),
        pltpu.VMEM((4, 2, B, D), bf),
        pltpu.VMEM((4, 2, B, D), bf),
        pltpu.VMEM((2 * B, D), bf),
        pltpu.VMEM((2 * B, D), bf),
        pltpu.VMEM((8, 16, B), jnp.int32),
        pltpu.VMEM((2 * B, B), f32),
        pltpu.VMEM((2 * B, B), f32),
        pltpu.VMEM((2 * B, D), f32),
        pltpu.VMEM((2 * B, D), f32),
        pltpu.VMEM((B, D), f32),
        pltpu.VMEM((B, D), f32),
        pltpu.VMEM((B, D), f32),
        pltpu.VMEM((D, B), bf),
        pltpu.VMEM((4, 2, 2, B, D), bf),
        pltpu.VMEM((SLICE, 16 * B), bf),
        pltpu.VMEM((9, SLICE, B), bf),
        pltpu.VMEM((16, SLICE, B), bf),
        pltpu.VMEM((SLICE, B), bf),
        dma((3,)),
    ]
    for n in (48, 7, 4, 21, 16):
        scratch += [dma((n,)), dma((n,))]
    scratch += [dma((9,)), dma((16,)), dma((8,)), dma((9,))]
    for n in (8, 8, 8):
        scratch += [dma((n,)), dma((n,))]
    scratch += [pltpu.VMEM((4, 2, 2, SLICE, D), bf), dma((8,))]
    gimg, gtxt, g = pl.pallas_call(
        kernel,
        out_shape=(
            jax.ShapeDtypeStruct((B, D), bf),
            jax.ShapeDtypeStruct((B, D), bf),
            jax.ShapeDtypeStruct((4, 2, 2, SLICE, D), bf),
        ),
        in_specs=[hbm, vmem, hbm, vmem, hbm],
        out_specs=(vmem, vmem, hbm),
        scratch_shapes=scratch,
        compiler_params=pltpu.CompilerParams(
            collective_id=0, has_side_effects=True, vmem_limit_bytes=60 * 2**20
        ),
    )(image_emb, image_ids.reshape(1, B), text_feats, text_ids.reshape(1, B), text_head)
    fixed = pl.BlockSpec((B, D), lambda n: (0, 0))
    return pl.pallas_call(
        finish,
        grid=(D // WIDE,),
        out_shape=(
            jax.ShapeDtypeStruct((B, D), bf),
            jax.ShapeDtypeStruct((B, D), bf),
            jax.ShapeDtypeStruct((D, D), f32),
        ),
        in_specs=[pl.BlockSpec((4, 2, 2, SLICE, WIDE), lambda n: (0, 0, 0, 0, n)), fixed, fixed],
        out_specs=(fixed, fixed, pl.BlockSpec((WIDE, D), lambda n: (n, 0))),
        scratch_shapes=[pltpu.VMEM((D, WIDE), bf)],
        compiler_params=pltpu.CompilerParams(vmem_limit_bytes=60 * 2**20),
    )(g, gimg, gtxt)


def solution(mesh):
    placed = (P("blk", None), P("blk"), P("blk", None), P("blk"), P())
    return jax.shard_map(
        shards,
        mesh=mesh,
        in_specs=placed,
        out_specs=(P("blk", None), P("blk", None), P()),
        check_vma=False,
    )
```

```python
import jax
import jax.numpy as jnp
from jax import lax
from jax.experimental import pallas as pl
from jax.experimental.pallas import tpu as pltpu
from jax.sharding import PartitionSpec as P

MESH = pl.DeviceIdType.MESH
D = 1152
B = 128
REACH = 6
SLICE = 80
OWNER = (0, 4, 8, 12, 2, 3, 7, 11, 15)
X_LANES = ((256, 384), (640, 256))
X_ALL = (256, 640)
WIDE = 384
NT = (((1,), (1,)), ((), ()))


def start_row(a):
    return pl.multiple_of(16 * ((9 * a) // 2), 16)


def kernel(
    img_hbm, imgid_ref, txt_hbm, txtid_ref, head_hbm,
    gimg_ref, gtxt_ref, g_ref,
    img_ref, txt_ref, head_ref, imgs, txts, img_pair, txt_pair, ids, img_col, txt_col,
    acc_t, acc_i, got_t, got_i, pre, gp_t, feats, gp_in, part, sums, block,
    load, band_s, band_r, id_s, id_r, pair_s, pair_r, f_s, f_r, gp_s, gp_r, rs_s, rs_r,
    az_s, az_r, a2_s, a2_r, a3_s, a3_r, am_s, am_r, g_vm, keep,
):
    loads = [
        pltpu.make_async_copy(a, b, load.at[n])
        for n, (a, b) in enumerate(
            ((img_hbm, img_ref), (txt_hbm, txt_ref), (head_hbm, head_ref))
        )
    ]
    for c in loads:
        c.start()

    me = lax.axis_index("blk")
    core = lax.rem(me, 2)
    z = lax.rem(me // 2, 8)
    x = lax.rem(me // 16, 4)
    y = me // 64
    g, xp = x // 2, lax.rem(x, 2)
    a = (y * 2 + xp) * 2 + core
    b = z * 2 + g

    def at(y2, x2, z2, c2):
        return ((y2 * 4 + x2) * 8 + z2) * 2 + c2

    def of_group(a2):
        return at(a2 // 4, 2 * g + lax.rem(a2 // 2, 2), z, lax.rem(a2, 2))

    def of_column(b2):
        return at(y, 2 * lax.rem(b2, 2) + xp, b2 // 2, core)

    mate = at(y, x, z, 1 - core)
    partner = at(y, x + 1 - 2 * xp, z, core)
    right, left = lax.rem(me + 2, 256), lax.rem(me + 254, 256)
    yp, ym, yo = lax.rem(y + 1, 4), lax.rem(y + 3, 4), lax.rem(y + 2, 4)
    up, down = at(yp, x, z, core), at(ym, x, z, core)

    barrier = pltpu.get_barrier_semaphore()

    def greet(device):
        pl.semaphore_signal(barrier, inc=1, device_id=(device,), device_id_type=MESH)

    for step in (2, 4, 6, 250, 252, 254):
        greet(lax.rem(me + step, 256))
    greet(at(y, 3 - x, z, core))

    def greet_groups(i, carry):
        greet(of_group(lax.rem(a + i, 16)))
        greet(of_column(lax.rem(b + i, 16)))
        return carry

    lax.fori_loop(1, 16, greet_groups, 0)

    sent = []

    def copy(src, dst, ssem, rsem, device):
        return pltpu.make_async_remote_copy(
            src_ref=src, dst_ref=dst, send_sem=ssem, recv_sem=rsem,
            device_id=(device,), device_id_type=MESH,
        )

    def send(src, dst, ssem, rsem, device):
        c = copy(src, dst, ssem, rsem, device)
        c.start()
        sent.append(c)
        return c

    loads[0].wait()
    image_f = img_ref[...].astype(jnp.float32)
    image_inv = lax.rsqrt(jnp.sum(image_f * image_f, axis=-1, keepdims=True) + 1e-06)
    own_z = (image_f * image_inv).astype(jnp.bfloat16)
    imgs[0, 0] = own_z
    img_pair[0:B] = own_z
    ids[0] = jnp.concatenate(
        [
            jnp.broadcast_to(imgid_ref[...], (8, B)),
            jnp.broadcast_to(txtid_ref[...], (8, B)),
        ],
        axis=0,
    )
    loads[1].wait()
    feats[y, xp, core] = txt_ref[...]

    pl.semaphore_wait(barrier, 37)

    hold = {}
    PARTS = (4, 2)

    def idle(kind, step, way):
        return step == 3 and way == kind

    def wanted(kind):
        return core == 1 if kind == 0 else core == 0

    def band_copy(kind, buf, step, way, n):
        rows = pl.ds(n * (B // PARTS[kind]), B // PARTS[kind])
        src = buf.at[0, 0, rows] if step == 1 else buf.at[step - 1, way, rows]
        k = ((kind * 2 + way) * 3 + step - 1) * 4 + n
        return copy(src, buf.at[step, way, rows], band_s.at[k], band_r.at[k], (right, left)[way])

    def band_send(kind, buf, step, way, n):
        if idle(kind, step, way):
            @pl.when(wanted(kind))
            def _():
                band_copy(kind, buf, step, way, n).start()
            return
        c = band_copy(kind, buf, step, way, n)
        c.start()
        sent.append(c)
        hold[kind, step, way, n] = c

    def band_start(kind, buf, first, last):
        for n in range(first, last):
            for way in range(2):
                band_send(kind, buf, 1, way, n)

    def band_pace(n):
        for way in range(2):
            c = hold[0, 1, way, n]
            c.wait_send()
            sent.remove(c)
            band_send(0, imgs, 1, way, n + 2)

    def band_forward(kind, buf, step):
        for n in range(PARTS[kind]):
            for way in range(2):
                hold[kind, step, way, n].wait_recv()
                band_send(kind, buf, step + 1, way, n)

    def band_wait(kind, buf, step):
        for n in range(PARTS[kind]):
            for way in range(2):
                if idle(kind, step, way):
                    @pl.when(wanted(kind))
                    def _():
                        band_copy(kind, buf, step, way, n).wait_recv()
                else:
                    hold[kind, step, way, n].wait_recv()

    band_start(0, imgs, 0, 2)
    id_copies = [send(ids.at[0], ids.at[7], id_s.at[6], id_r.at[6], mate)]
    for n, step in enumerate((2, 4, 6)):
        for way in range(2):
            k = 2 * n + way
            to = lax.rem(me + (step if way == 0 else 256 - step), 256)
            id_copies.append(send(ids.at[0], ids.at[1 + k], id_s.at[k], id_r.at[k], to))

    F = {}

    def feat_copy(k, y2, xp2, device, rows=pl.ds(0, B), arrival=None):
        view = feats.at[y2, xp2, core, rows]
        return copy(view, view, f_s.at[k], f_r.at[k if arrival is None else arrival], device)

    def feat_send(name, *place):
        F[name] = feat_copy(*place)
        F[name].start()
        sent.append(F[name])

    maybe = []

    def feat_when(cond, name, *place):
        c = F[name] = feat_copy(*place)

        @pl.when(cond)
        def _():
            c.start()

        maybe.append((cond, c))

    up_shut, up_help = (x == 0) & (z == 0), (x == 1) & (z == 0)
    down_shut, down_help = (x == 3) & (z == 7), (x == 2) & (z == 7)
    up_open, down_open = jnp.logical_not(up_shut), jnp.logical_not(down_shut)
    other = 1 - xp
    feat_send("x", 0, y, xp, partner)
    feat_when(up_open, "u", 1, y, xp, up)
    feat_when(down_open, "d", 2, y, xp, down)
    img_mate = send(imgs.at[0, 0], img_pair.at[pl.ds(B, B)], pair_s.at[0], pair_r.at[0], mate)
    feat_send("m0", 8 + 0, y, xp, mate)

    low, high = pl.ds(0, B // 2), pl.ds(B // 2, B // 2)

    def feats_second():
        F["x"].wait_recv()
        feat_when(up_open, "xu", 3, y, other, up)
        feat_when(down_open, "xd", 4, y, other, down)
        feat_send("m1", 8 + 1, y, other, mate)

    def feats_up():
        F["u"].wait_recv()
        F["xu"].wait_recv()
        F["m2"].start()
        F["m4"].start()

    def feats_down():
        F["d"].wait_recv()
        F["xd"].wait_recv()
        F["m3"].start()
        F["m5"].start()

    def feats_third():
        for k, y2, xp2 in ((2, ym, xp), (3, yp, xp), (4, ym, other), (5, yp, other)):
            F["m%d" % k] = feat_copy(8 + k, y2, xp2, mate)
            sent.append(F["m%d" % k])
        pl.when(up_open)(feats_up)
        pl.when(down_open)(feats_down)
        low_from, low_to = jnp.where(up_shut, yp, ym), jnp.where(up_shut, down, up)
        high_from, high_to = jnp.where(down_shut, ym, yp), jnp.where(down_shut, up, down)
        feat_send("o0", 5, low_from, xp, low_to, low)
        feat_send("o1", 6, high_from, xp, high_to, high)
        feat_send("xo0", 7, low_from, other, low_to, low)
        feat_send("xo1", 16, high_from, other, high_to, high)
        feat_when(up_help, "hu0", 17, ym, xp, partner, pl.ds(0, B), 3)
        feat_when(up_help, "hu1", 18, ym, other, partner, pl.ds(0, B), 1)
        feat_when(down_help, "hd0", 19, yp, xp, partner, pl.ds(0, B), 4)
        feat_when(down_help, "hd1", 20, yp, other, partner, pl.ds(0, B), 2)

    def feats_fourth():
        F["o0"].wait_recv()
        F["o1"].wait_recv()
        feat_send("m6", 8 + 6, yo, xp, mate)
        F["xo0"].wait_recv()
        F["xo1"].wait_recv()
        feat_send("m7", 8 + 7, yo, other, mate)
        pl.when(up_shut)(feats_up)
        pl.when(down_shut)(feats_down)

    def feats_wait():
        for n in range(8):
            F["m%d" % n].wait_recv()

    @pl.when(core == 0)
    def _():
        imgs[3, 0] = jnp.zeros((B, D), jnp.bfloat16)

    @pl.when(core == 1)
    def _():
        txts[3, 1] = jnp.zeros((B, D), jnp.bfloat16)

    loads[2].wait()
    pre[...] = jnp.dot(txt_ref[...], head_ref[...], preferred_element_type=jnp.float32)
    text_pre = pre[...]
    text_inv = lax.rsqrt(jnp.sum(text_pre * text_pre, axis=-1, keepdims=True) + 1e-06)
    text_z = (text_pre * text_inv).astype(jnp.bfloat16)
    txts[0, 0] = text_z
    txt_pair[0:B] = text_z
    txt_mate = send(txts.at[0, 0], txt_pair.at[pl.ds(B, B)], pair_s.at[1], pair_r.at[1], mate)

    for c in id_copies:
        c.wait_recv()

    def column(row):
        return jnp.transpose(jnp.broadcast_to(row.astype(jnp.float32), (B, B)))

    for h, slot in ((0, 0), (1, 7)):
        img_col[pl.ds(h * B, B)] = column(ids[slot, 0:1])
        txt_col[pl.ds(h * B, B)] = column(ids[slot, 8:9])

    def process(kind, step, here_ref, col_ref, blocks, acc_ref):
        slots = (0,) if step == 0 else (2 * step - 1, 2 * step)
        logit = (
            10.0 * lax.dot_general(here_ref[...], blocks, NT, preferred_element_type=jnp.float32)
            - 5.0
        )
        coefs = []
        for n, slot in enumerate(slots):
            row = ids[slot, 8 * kind : 8 * kind + 1].astype(jnp.float32)
            label = jnp.where(col_ref[...] == row, 1.0, -1.0)
            part_logit = logit[:, n * B : (n + 1) * B]
            coef = -label * jax.nn.sigmoid(-label * part_logit)
            if step == 3:
                delta = 2 * step * (2 * n - 1)
                offset = (delta, delta + 2 * core - 1) if kind == 0 else (-delta, 1 - 2 * core - delta)
                keep = [
                    jnp.where((o >= 1 - REACH) & (o <= REACH), 1.0, 0.0).astype(jnp.float32)
                    for o in offset
                ]
                half = lax.broadcasted_iota(jnp.int32, coef.shape, 0) < B
                coef = coef * jnp.where(half, keep[0], keep[1])
            coefs.append(coef.astype(jnp.bfloat16))
        coef = coefs[0] if len(coefs) == 1 else jnp.concatenate(coefs, axis=1)
        term = jnp.dot(coef, blocks, preferred_element_type=jnp.float32)
        if step == 0:
            acc_ref[...] = term
        else:
            acc_ref[...] += term

    def pair_block(buf, step):
        return buf[step].reshape(2 * B, D)

    def process_images(step):
        process(0, step, txt_pair, txt_col, pair_block(imgs, step), acc_t)

    def process_texts(step):
        process(1, step, img_pair, img_col, pair_block(txts, step), acc_i)

    band_pace(0)
    txt_mate.wait_recv()
    process(0, 0, txt_pair, txt_col, imgs[0, 0], acc_t)
    band_pace(1)
    img_mate.wait_recv()
    process(1, 0, img_pair, img_col, txts[0, 0], acc_i)
    band_forward(0, imgs, 1)
    feats_second()
    process_images(1)
    band_forward(0, imgs, 2)
    feats_third()
    process_images(2)
    band_wait(0, imgs, 3)
    band_start(1, txts, 0, 2)
    process_images(3)
    swap = send(acc_t.at[pl.ds(B, B)], got_t, pair_s.at[2], pair_r.at[2], mate)
    text_unit = pre[...] * text_inv
    swap.wait_recv()
    grad_tz = 10.0 * (acc_t[0:B] + got_t[...])
    grad_pre = (
        grad_tz - text_unit * jnp.sum(text_unit * grad_tz, axis=-1, keepdims=True)
    ) * text_inv
    for n in range(9):
        gp_t[n * B : (n + 1) * B] = jnp.transpose(grad_pre[:, n * B : (n + 1) * B]).astype(
            jnp.bfloat16
        )
    grad_pre = grad_pre.astype(jnp.bfloat16)

    def gp_copy(i):
        a2 = lax.rem(a + i, 16)
        return copy(
            gp_t.at[pl.ds(start_row(a2), SLICE)],
            gp_in.at[:, pl.ds(pl.multiple_of(a * B, B), B)],
            gp_s.at[i], gp_r.at[i], of_group(a2),
        )

    def gp_send(i, carry):
        gp_copy(i).start()
        return carry

    lax.fori_loop(1, 16, gp_send, 0)
    gp_in[:, pl.ds(pl.multiple_of(a * B, B), B)] = gp_t[pl.ds(start_row(a), SLICE)]
    band_forward(1, txts, 1)
    feats_fourth()
    gtxt_ref[...] = lax.dot_general(
        grad_pre, head_ref[...], NT, preferred_element_type=jnp.float32
    ).astype(jnp.bfloat16)
    process_texts(1)
    feats_wait()

    def gp_wait(i, carry):
        gp_copy(i).wait_recv()
        return carry

    lax.fori_loop(1, 16, gp_wait, 0)
    def rs_copy(n, to):
        return copy(part.at[n], sums.at[b], rs_s.at[n], rs_r.at[b], of_column(to))

    for first in range(0, 9, 2):
        blocks = range(first, min(first + 2, 9))
        columns = feats[:, :, :, :, first * B : blocks.stop * B].reshape(16 * B, len(blocks) * B)
        slices = jnp.dot(gp_in[...], columns, preferred_element_type=jnp.float32)
        for n in blocks:
            part[n] = slices[:, (n - first) * B : (n - first + 1) * B].astype(jnp.bfloat16)

            @pl.when(b != OWNER[n])
            def _():
                rs_copy(n, OWNER[n]).start()

            @pl.when(b == OWNER[n])
            def _():
                sums[b] = part[n]

    band_forward(1, txts, 2)
    mine = jnp.where(g == 0, jnp.where(b == 2, 4, z // 2), 5 + z // 2)
    is_owner = jnp.logical_or(lax.rem(z, 2) == g, b == 2)
    lanes = pl.ds(pl.multiple_of(mine * B, B), B)

    def az_copy(i):
        return copy(
            block, g_vm.at[y, xp, core, :, lanes], az_s.at[i], az_r.at[mine],
            at(y, x, lax.rem(z + i, 8), core),
        )

    @pl.when(is_owner)
    def _():
        def rs_wait(i, carry):
            b2 = lax.rem(b + i, 16)
            copy(part.at[0], sums.at[b2], rs_s.at[0], rs_r.at[b2], mate).wait_recv()
            return carry

        lax.fori_loop(1, 16, rs_wait, 0)
        total = sums[0].astype(jnp.float32)
        for n in range(1, 16):
            total = total + sums[n].astype(jnp.float32)
        block[...] = total.astype(jnp.bfloat16)
        g_vm[y, xp, core, :, lanes] = total.astype(jnp.bfloat16)

        def az_send(i, carry):
            az_copy(i).start()
            return carry

        lax.fori_loop(1, 8, az_send, 0)

    for gg, (first, count) in enumerate(((0, 5), (5, 4))):
        for n in range(first, first + count):
            @pl.when((g == gg) & (b != OWNER[n]))
            def _():
                copy(
                    block, g_vm.at[y, xp, core, :, pl.ds(n * B, B)], az_s.at[0], az_r.at[n], mate
                ).wait_recv()

    def lanes_y(g2):
        return pl.ds(pl.multiple_of(896 * g2, B), 256)

    def back(x2, i):
        return lax.rem(x2 + 4 - i, 4)

    def along_x(i):
        return at(y, lax.rem(x + i, 4), z, core)

    def along_y(i):
        return at(lax.rem(y + i, 4), x, z, core)

    def second_x(i, gg):
        view = g_vm.at[y, xp, core, :, pl.ds(*X_LANES[gg])]
        return copy(view, view, a2_s.at[i], a2_r.at[i], along_x(i))

    def second_y(i):
        view = g_vm.at[y, xp, core, :, lanes_y(g)]
        return copy(view, view, a2_s.at[4 + i], a2_r.at[4 + i], along_y(i))

    def third_x(i):
        view = g_vm.at[y, :, core, :, pl.ds(*X_ALL)]
        return copy(view, view, a3_s.at[i], a3_r.at[i], along_y(i))

    def third_y(i):
        view = g_vm.at[:, xp, core, :, lanes_y(g)]
        return copy(view, view, a3_s.at[4 + i], a3_r.at[4 + i], along_x(i))

    def place_x(ref, i, c2):
        return ref.at[back(y, i), :, c2, :, pl.ds(*X_ALL)]

    def place_y(ref, i, c2):
        x2 = back(x, i)
        return ref.at[:, lax.rem(x2, 2), c2, :, lanes_y(x2 // 2)]

    def mate_x(i, c2):
        return copy(place_x(g_vm, i, c2), place_x(g_ref, i, c2), am_s.at[i], am_r.at[i], mate)

    def mate_y(i, c2):
        return copy(
            place_y(g_vm, i, c2), place_y(g_ref, i, c2), am_s.at[4 + i], am_r.at[4 + i], mate
        )

    def keep_x(i):
        return pltpu.make_async_copy(place_x(g_vm, i, core), place_x(g_ref, i, core), keep.at[i])

    def keep_y(i):
        return pltpu.make_async_copy(
            place_y(g_vm, i, core), place_y(g_ref, i, core), keep.at[4 + i]
        )

    ORDER = (1, 3, 2)
    for i in ORDER:
        for gg in range(2):
            @pl.when(g == gg)
            def _():
                second_x(i, gg).start()
        second_y(i).start()
    for i in ORDER:
        for gg in range(2):
            @pl.when(back(x, i) // 2 == gg)
            def _():
                second_x(i, gg).wait_recv()
    for i in ORDER:
        third_x(i).start()
    for i in ORDER:
        second_y(i).wait_recv()
    for i in ORDER:
        third_y(i).start()
    mate_x(0, core).start()
    keep_x(0).start()
    mate_y(0, core).start()
    keep_y(0).start()


    process_texts(2)
    band_wait(1, txts, 3)
    process_texts(3)
    swap_i = send(acc_i.at[pl.ds(B, B)], got_i, pair_s.at[3], pair_r.at[3], mate)
    third_x(1).wait_recv()
    mate_x(1, core).start()
    keep_x(1).start()
    third_y(1).wait_recv()
    mate_y(1, core).start()
    keep_y(1).start()
    third_x(3).wait_recv()
    mate_x(3, core).start()
    keep_x(3).start()
    third_y(3).wait_recv()
    mate_y(3, core).start()
    keep_y(3).start()
    third_x(2).wait_recv()
    mate_x(2, core).start()
    keep_x(2).start()
    third_y(2).wait_recv()
    mate_y(2, core).start()
    keep_y(2).start()
    swap_i.wait_recv()
    grad_iz = 10.0 * (acc_i[0:B] + got_i[...])
    image_g = img_ref[...].astype(jnp.float32)
    image_unit = image_g * image_inv
    gimg_ref[...] = (
        (grad_iz - image_unit * jnp.sum(image_unit * grad_iz, axis=-1, keepdims=True)) * image_inv
    ).astype(jnp.bfloat16)

    for cond, c in maybe:
        pl.when(cond)(c.wait_send)
    for kind, buf in ((0, imgs), (1, txts)):
        @pl.when(wanted(kind))
        def _():
            for n in range(PARTS[kind]):
                band_copy(kind, buf, 3, kind, n).wait_send()
    for c in sent:
        c.wait_send()

    def gp_drain(i, carry):
        gp_copy(i).wait_send()
        return carry

    lax.fori_loop(1, 16, gp_drain, 0)
    for n, to in enumerate(OWNER):
        @pl.when(b != to)
        def _():
            rs_copy(n, to).wait_send()

    @pl.when(is_owner)
    def _():
        def az_drain(i, carry):
            az_copy(i).wait_send()
            return carry

        lax.fori_loop(1, 8, az_drain, 0)

    for i in ORDER:
        for gg in range(2):
            @pl.when(g == gg)
            def _():
                second_x(i, gg).wait_send()
        second_y(i).wait_send()
        third_x(i).wait_send()
        third_y(i).wait_send()
    for i in range(4):
        keep_x(i).wait()
        keep_y(i).wait()
        mate_x(i, core).wait_send()
        mate_y(i, core).wait_send()
        mate_x(i, 1 - core).wait_recv()
        mate_y(i, 1 - core).wait_recv()


def finish(g_ref, gimg_ref, gtxt_ref, oimg_ref, otxt_ref, ohead_ref, whole):
    @pl.when(pl.program_id(0) == 0)
    def _():
        oimg_ref[...] = gimg_ref[...]
        otxt_ref[...] = gtxt_ref[...]

    for a in range(16):
        view = g_ref[a // 4, (a // 2) % 2, a % 2]
        if a % 2 == 0:
            whole[72 * a : 72 * a + 80] = view
        else:
            whole[72 * a + 8 : 72 * a + 72] = view[16:80]
    for start, size in ((0, 256), (256, 128)):
        eye = lax.broadcasted_iota(jnp.int32, (size, size), 0) == lax.broadcasted_iota(
            jnp.int32, (size, size), 1
        )
        ohead_ref[start : start + size] = lax.dot_general(
            eye.astype(jnp.bfloat16), whole[:, start : start + size], NT,
            preferred_element_type=jnp.float32,
        )


def shards(image_emb, image_ids, text_feats, text_ids, text_head):
    bf, f32 = jnp.bfloat16, jnp.float32
    vmem = pl.BlockSpec(memory_space=pltpu.VMEM)
    hbm = pl.BlockSpec(memory_space=pl.ANY)
    dma = pltpu.SemaphoreType.DMA
    scratch = [
        pltpu.VMEM((B, D), bf),
        pltpu.VMEM((B, D), bf),
        pltpu.VMEM((D, D), bf),
        pltpu.VMEM((4, 2, B, D), bf),
        pltpu.VMEM((4, 2, B, D), bf),
        pltpu.VMEM((2 * B, D), bf),
        pltpu.VMEM((2 * B, D), bf),
        pltpu.VMEM((8, 16, B), jnp.int32),
        pltpu.VMEM((2 * B, B), f32),
        pltpu.VMEM((2 * B, B), f32),
        pltpu.VMEM((2 * B, D), f32),
        pltpu.VMEM((2 * B, D), f32),
        pltpu.VMEM((B, D), f32),
        pltpu.VMEM((B, D), f32),
        pltpu.VMEM((B, D), f32),
        pltpu.VMEM((D, B), bf),
        pltpu.VMEM((4, 2, 2, B, D), bf),
        pltpu.VMEM((SLICE, 16 * B), bf),
        pltpu.VMEM((9, SLICE, B), bf),
        pltpu.VMEM((16, SLICE, B), bf),
        pltpu.VMEM((SLICE, B), bf),
        dma((3,)),
    ]
    for n in (48, 7, 4, 21, 16):
        scratch += [dma((n,)), dma((n,))]
    scratch += [dma((9,)), dma((16,)), dma((8,)), dma((9,))]
    for n in (8, 8, 8):
        scratch += [dma((n,)), dma((n,))]
    scratch += [pltpu.VMEM((4, 2, 2, SLICE, D), bf), dma((8,))]
    gimg, gtxt, g = pl.pallas_call(
        kernel,
        out_shape=(
            jax.ShapeDtypeStruct((B, D), bf),
            jax.ShapeDtypeStruct((B, D), bf),
            jax.ShapeDtypeStruct((4, 2, 2, SLICE, D), bf),
        ),
        in_specs=[hbm, vmem, hbm, vmem, hbm],
        out_specs=(vmem, vmem, hbm),
        scratch_shapes=scratch,
        compiler_params=pltpu.CompilerParams(
            collective_id=0, has_side_effects=True, vmem_limit_bytes=60 * 2**20
        ),
    )(image_emb, image_ids.reshape(1, B), text_feats, text_ids.reshape(1, B), text_head)
    fixed = pl.BlockSpec((B, D), lambda n: (0, 0))
    return pl.pallas_call(
        finish,
        grid=(D // WIDE,),
        out_shape=(
            jax.ShapeDtypeStruct((B, D), bf),
            jax.ShapeDtypeStruct((B, D), bf),
            jax.ShapeDtypeStruct((D, D), f32),
        ),
        in_specs=[pl.BlockSpec((4, 2, 2, SLICE, WIDE), lambda n: (0, 0, 0, 0, n)), fixed, fixed],
        out_specs=(fixed, fixed, pl.BlockSpec((WIDE, D), lambda n: (n, 0))),
        scratch_shapes=[pltpu.VMEM((D, WIDE), bf)],
        compiler_params=pltpu.CompilerParams(vmem_limit_bytes=60 * 2**20),
    )(g, gimg, gtxt)


def solution(mesh):
    placed = (P("blk", None), P("blk"), P("blk", None), P("blk"), P())
    return jax.shard_map(
        shards,
        mesh=mesh,
        in_specs=placed,
        out_specs=(P("blk", None), P("blk", None), P()),
        check_vma=False,
    )
```

```python
import jax
import jax.numpy as jnp
from jax import lax
from jax.experimental import pallas as pl
from jax.experimental.pallas import tpu as pltpu
from jax.sharding import PartitionSpec as P

MESH = pl.DeviceIdType.MESH
D = 1152
B = 128
REACH = 6
SLICE = 80
OWNER = (0, 4, 8, 12, 2, 3, 7, 11, 15)
X_LANES = ((256, 384), (640, 256))
X_ALL = (256, 640)
WIDE = 384
NT = (((1,), (1,)), ((), ()))


def start_row(a):
    return pl.multiple_of(16 * ((9 * a) // 2), 16)


def kernel(
    img_hbm, imgid_ref, txt_hbm, txtid_ref, head_hbm,
    gimg_ref, gtxt_ref, g_ref,
    img_ref, txt_ref, head_ref, imgs, txts, img_pair, txt_pair, ids, img_col, txt_col,
    acc_t, acc_i, got_t, got_i, pre, gp_t, feats, gp_in, part, sums, block,
    load, band_s, band_r, id_s, id_r, pair_s, pair_r, f_s, f_r, gp_s, gp_r, rs_s, rs_r,
    az_s, az_r, a2_s, a2_r, a3_s, a3_r, am_s, am_r, g_vm, keep,
):
    loads = [
        pltpu.make_async_copy(a, b, load.at[n])
        for n, (a, b) in enumerate(
            ((img_hbm, img_ref), (txt_hbm, txt_ref), (head_hbm, head_ref))
        )
    ]
    for c in loads:
        c.start()

    me = lax.axis_index("blk")
    core = lax.rem(me, 2)
    z = lax.rem(me // 2, 8)
    x = lax.rem(me // 16, 4)
    y = me // 64
    g, xp = x // 2, lax.rem(x, 2)
    a = (y * 2 + xp) * 2 + core
    b = z * 2 + g

    def at(y2, x2, z2, c2):
        return ((y2 * 4 + x2) * 8 + z2) * 2 + c2

    def of_group(a2):
        return at(a2 // 4, 2 * g + lax.rem(a2 // 2, 2), z, lax.rem(a2, 2))

    def of_column(b2):
        return at(y, 2 * lax.rem(b2, 2) + xp, b2 // 2, core)

    mate = at(y, x, z, 1 - core)
    partner = at(y, x + 1 - 2 * xp, z, core)
    right, left = lax.rem(me + 2, 256), lax.rem(me + 254, 256)
    yp, ym, yo = lax.rem(y + 1, 4), lax.rem(y + 3, 4), lax.rem(y + 2, 4)
    up, down = at(yp, x, z, core), at(ym, x, z, core)

    barrier = pltpu.get_barrier_semaphore()

    def greet(device):
        pl.semaphore_signal(barrier, inc=1, device_id=(device,), device_id_type=MESH)

    for step in (2, 4, 6, 250, 252, 254):
        greet(lax.rem(me + step, 256))
    greet(at(y, 3 - x, z, core))

    def greet_groups(i, carry):
        greet(of_group(lax.rem(a + i, 16)))
        greet(of_column(lax.rem(b + i, 16)))
        return carry

    lax.fori_loop(1, 16, greet_groups, 0)

    sent = []

    def copy(src, dst, ssem, rsem, device):
        return pltpu.make_async_remote_copy(
            src_ref=src, dst_ref=dst, send_sem=ssem, recv_sem=rsem,
            device_id=(device,), device_id_type=MESH,
        )

    def send(src, dst, ssem, rsem, device):
        c = copy(src, dst, ssem, rsem, device)
        c.start()
        sent.append(c)
        return c

    loads[0].wait()
    image_f = img_ref[...].astype(jnp.float32)
    image_inv = lax.rsqrt(jnp.sum(image_f * image_f, axis=-1, keepdims=True) + 1e-06)
    own_z = (image_f * image_inv).astype(jnp.bfloat16)
    imgs[0, 0] = own_z
    img_pair[0:B] = own_z
    ids[0] = jnp.concatenate(
        [
            jnp.broadcast_to(imgid_ref[...], (8, B)),
            jnp.broadcast_to(txtid_ref[...], (8, B)),
        ],
        axis=0,
    )
    loads[1].wait()
    feats[y, xp, core] = txt_ref[...]

    pl.semaphore_wait(barrier, 37)

    hold = {}
    PARTS = (4, 2)

    def idle(kind, step, way):
        return step == 3 and way == kind

    def wanted(kind):
        return core == 1 if kind == 0 else core == 0

    def band_copy(kind, buf, step, way, n):
        rows = pl.ds(n * (B // PARTS[kind]), B // PARTS[kind])
        src = buf.at[0, 0, rows] if step == 1 else buf.at[step - 1, way, rows]
        k = ((kind * 2 + way) * 3 + step - 1) * 4 + n
        return copy(src, buf.at[step, way, rows], band_s.at[k], band_r.at[k], (right, left)[way])

    def band_send(kind, buf, step, way, n):
        if idle(kind, step, way):
            @pl.when(wanted(kind))
            def _():
                band_copy(kind, buf, step, way, n).start()
            return
        c = band_copy(kind, buf, step, way, n)
        c.start()
        sent.append(c)
        hold[kind, step, way, n] = c

    def band_start(kind, buf, first, last):
        for n in range(first, last):
            for way in range(2):
                band_send(kind, buf, 1, way, n)

    def band_pace(n):
        for way in range(2):
            c = hold[0, 1, way, n]
            c.wait_send()
            sent.remove(c)
            band_send(0, imgs, 1, way, n + 2)

    def band_forward(kind, buf, step):
        for n in range(PARTS[kind]):
            for way in range(2):
                hold[kind, step, way, n].wait_recv()
                band_send(kind, buf, step + 1, way, n)

    def band_wait(kind, buf, step):
        for n in range(PARTS[kind]):
            for way in range(2):
                if idle(kind, step, way):
                    @pl.when(wanted(kind))
                    def _():
                        band_copy(kind, buf, step, way, n).wait_recv()
                else:
                    hold[kind, step, way, n].wait_recv()

    band_start(0, imgs, 0, 2)
    id_copies = [send(ids.at[0], ids.at[7], id_s.at[6], id_r.at[6], mate)]
    for n, step in enumerate((2, 4, 6)):
        for way in range(2):
            k = 2 * n + way
            to = lax.rem(me + (step if way == 0 else 256 - step), 256)
            id_copies.append(send(ids.at[0], ids.at[1 + k], id_s.at[k], id_r.at[k], to))

    F = {}

    def feat_copy(k, y2, xp2, device, rows=pl.ds(0, B), arrival=None):
        view = feats.at[y2, xp2, core, rows]
        return copy(view, view, f_s.at[k], f_r.at[k if arrival is None else arrival], device)

    def feat_send(name, *place):
        F[name] = feat_copy(*place)
        F[name].start()
        sent.append(F[name])

    maybe = []

    def feat_when(cond, name, *place):
        c = F[name] = feat_copy(*place)

        @pl.when(cond)
        def _():
            c.start()

        maybe.append((cond, c))

    up_shut, up_help = (x == 0) & (z == 0), (x == 1) & (z == 0)
    down_shut, down_help = (x == 3) & (z == 7), (x == 2) & (z == 7)
    up_open, down_open = jnp.logical_not(up_shut), jnp.logical_not(down_shut)
    other = 1 - xp
    feat_send("x", 0, y, xp, partner)
    feat_when(up_open, "u", 1, y, xp, up)
    feat_when(down_open, "d", 2, y, xp, down)
    img_mate = send(imgs.at[0, 0], img_pair.at[pl.ds(B, B)], pair_s.at[0], pair_r.at[0], mate)
    feat_send("m0", 8 + 0, y, xp, mate)

    low, high = pl.ds(0, B // 2), pl.ds(B // 2, B // 2)

    def feats_second():
        F["x"].wait_recv()
        feat_when(up_open, "xu", 3, y, other, up)
        feat_when(down_open, "xd", 4, y, other, down)
        feat_send("m1", 8 + 1, y, other, mate)

    def feats_up():
        F["u"].wait_recv()
        F["xu"].wait_recv()
        F["m2"].start()
        F["m4"].start()

    def feats_down():
        F["d"].wait_recv()
        F["xd"].wait_recv()
        F["m3"].start()
        F["m5"].start()

    def feats_third():
        for k, y2, xp2 in ((2, ym, xp), (3, yp, xp), (4, ym, other), (5, yp, other)):
            F["m%d" % k] = feat_copy(8 + k, y2, xp2, mate)
            sent.append(F["m%d" % k])
        pl.when(up_open)(feats_up)
        pl.when(down_open)(feats_down)
        low_from, low_to = jnp.where(up_shut, yp, ym), jnp.where(up_shut, down, up)
        high_from, high_to = jnp.where(down_shut, ym, yp), jnp.where(down_shut, up, down)
        feat_send("o0", 5, low_from, xp, low_to, low)
        feat_send("o1", 6, high_from, xp, high_to, high)
        feat_send("xo0", 7, low_from, other, low_to, low)
        feat_send("xo1", 16, high_from, other, high_to, high)
        feat_when(up_help, "hu0", 17, ym, xp, partner, pl.ds(0, B), 3)
        feat_when(up_help, "hu1", 18, ym, other, partner, pl.ds(0, B), 1)
        feat_when(down_help, "hd0", 19, yp, xp, partner, pl.ds(0, B), 4)
        feat_when(down_help, "hd1", 20, yp, other, partner, pl.ds(0, B), 2)

    def feats_fourth():
        F["o0"].wait_recv()
        F["o1"].wait_recv()
        feat_send("m6", 8 + 6, yo, xp, mate)
        F["xo0"].wait_recv()
        F["xo1"].wait_recv()
        feat_send("m7", 8 + 7, yo, other, mate)
        pl.when(up_shut)(feats_up)
        pl.when(down_shut)(feats_down)

    def feats_wait():
        for n in range(8):
            F["m%d" % n].wait_recv()

    @pl.when(core == 0)
    def _():
        imgs[3, 0] = jnp.zeros((B, D), jnp.bfloat16)

    @pl.when(core == 1)
    def _():
        txts[3, 1] = jnp.zeros((B, D), jnp.bfloat16)

    loads[2].wait()
    pre[...] = jnp.dot(txt_ref[...], head_ref[...], preferred_element_type=jnp.float32)
    text_pre = pre[...]
    text_inv = lax.rsqrt(jnp.sum(text_pre * text_pre, axis=-1, keepdims=True) + 1e-06)
    text_z = (text_pre * text_inv).astype(jnp.bfloat16)
    txts[0, 0] = text_z
    txt_pair[0:B] = text_z
    txt_mate = send(txts.at[0, 0], txt_pair.at[pl.ds(B, B)], pair_s.at[1], pair_r.at[1], mate)

    for c in id_copies:
        c.wait_recv()

    def column(row):
        return jnp.transpose(jnp.broadcast_to(row.astype(jnp.float32), (B, B)))

    for h, slot in ((0, 0), (1, 7)):
        img_col[pl.ds(h * B, B)] = column(ids[slot, 0:1])
        txt_col[pl.ds(h * B, B)] = column(ids[slot, 8:9])

    def process(kind, step, here_ref, col_ref, blocks, acc_ref):
        slots = (0,) if step == 0 else (2 * step - 1, 2 * step)
        logit = (
            10.0 * lax.dot_general(here_ref[...], blocks, NT, preferred_element_type=jnp.float32)
            - 5.0
        )
        coefs = []
        for n, slot in enumerate(slots):
            row = ids[slot, 8 * kind : 8 * kind + 1].astype(jnp.float32)
            label = jnp.where(col_ref[...] == row, 1.0, -1.0)
            part_logit = logit[:, n * B : (n + 1) * B]
            coef = -label * jax.nn.sigmoid(-label * part_logit)
            if step == 3:
                delta = 2 * step * (2 * n - 1)
                offset = (delta, delta + 2 * core - 1) if kind == 0 else (-delta, 1 - 2 * core - delta)
                keep = [
                    jnp.where((o >= 1 - REACH) & (o <= REACH), 1.0, 0.0).astype(jnp.float32)
                    for o in offset
                ]
                half = lax.broadcasted_iota(jnp.int32, coef.shape, 0) < B
                coef = coef * jnp.where(half, keep[0], keep[1])
            coefs.append(coef.astype(jnp.bfloat16))
        coef = coefs[0] if len(coefs) == 1 else jnp.concatenate(coefs, axis=1)
        term = jnp.dot(coef, blocks, preferred_element_type=jnp.float32)
        if step == 0:
            acc_ref[...] = term
        else:
            acc_ref[...] += term

    def pair_block(buf, step):
        return buf[step].reshape(2 * B, D)

    def process_images(step):
        process(0, step, txt_pair, txt_col, pair_block(imgs, step), acc_t)

    def process_texts(step):
        process(1, step, img_pair, img_col, pair_block(txts, step), acc_i)

    band_pace(0)
    txt_mate.wait_recv()
    process(0, 0, txt_pair, txt_col, imgs[0, 0], acc_t)
    band_pace(1)
    img_mate.wait_recv()
    process(1, 0, img_pair, img_col, txts[0, 0], acc_i)
    band_forward(0, imgs, 1)
    feats_second()
    process_images(1)
    band_forward(0, imgs, 2)
    feats_third()
    process_images(2)
    band_wait(0, imgs, 3)
    band_start(1, txts, 0, 2)
    process_images(3)
    swap = send(acc_t.at[pl.ds(B, B)], got_t, pair_s.at[2], pair_r.at[2], mate)
    text_unit = pre[...] * text_inv
    swap.wait_recv()
    grad_tz = 10.0 * (acc_t[0:B] + got_t[...])
    grad_pre = (
        grad_tz - text_unit * jnp.sum(text_unit * grad_tz, axis=-1, keepdims=True)
    ) * text_inv
    for n in range(9):
        gp_t[n * B : (n + 1) * B] = jnp.transpose(grad_pre[:, n * B : (n + 1) * B]).astype(
            jnp.bfloat16
        )
    grad_pre = grad_pre.astype(jnp.bfloat16)

    def gp_copy(i):
        a2 = lax.rem(a + i, 16)
        return copy(
            gp_t.at[pl.ds(start_row(a2), SLICE)],
            gp_in.at[:, pl.ds(pl.multiple_of(a * B, B), B)],
            gp_s.at[i], gp_r.at[i], of_group(a2),
        )

    def gp_send(i, carry):
        gp_copy(i).start()
        return carry

    lax.fori_loop(1, 16, gp_send, 0)
    gp_in[:, pl.ds(pl.multiple_of(a * B, B), B)] = gp_t[pl.ds(start_row(a), SLICE)]
    band_forward(1, txts, 1)
    feats_fourth()
    process_texts(1)
    feats_wait()

    def gp_wait(i, carry):
        gp_copy(i).wait_recv()
        return carry

    lax.fori_loop(1, 16, gp_wait, 0)
    def rs_copy(n, to):
        return copy(part.at[n], sums.at[b], rs_s.at[n], rs_r.at[b], of_column(to))

    for first in range(0, 9, 2):
        blocks = range(first, min(first + 2, 9))
        columns = feats[:, :, :, :, first * B : blocks.stop * B].reshape(16 * B, len(blocks) * B)
        slices = jnp.dot(gp_in[...], columns, preferred_element_type=jnp.float32)
        for n in blocks:
            part[n] = slices[:, (n - first) * B : (n - first + 1) * B].astype(jnp.bfloat16)

            @pl.when(b != OWNER[n])
            def _():
                rs_copy(n, OWNER[n]).start()

            @pl.when(b == OWNER[n])
            def _():
                sums[b] = part[n]

    band_forward(1, txts, 2)
    mine = jnp.where(g == 0, jnp.where(b == 2, 4, z // 2), 5 + z // 2)
    is_owner = jnp.logical_or(lax.rem(z, 2) == g, b == 2)
    lanes = pl.ds(pl.multiple_of(mine * B, B), B)

    def az_copy(i):
        return copy(
            block, g_vm.at[y, xp, core, :, lanes], az_s.at[i], az_r.at[mine],
            at(y, x, lax.rem(z + i, 8), core),
        )

    @pl.when(is_owner)
    def _():
        def rs_wait(i, carry):
            b2 = lax.rem(b + i, 16)
            copy(part.at[0], sums.at[b2], rs_s.at[0], rs_r.at[b2], mate).wait_recv()
            return carry

        lax.fori_loop(1, 16, rs_wait, 0)
        total = sums[0].astype(jnp.float32)
        for n in range(1, 16):
            total = total + sums[n].astype(jnp.float32)
        block[...] = total.astype(jnp.bfloat16)
        g_vm[y, xp, core, :, lanes] = total.astype(jnp.bfloat16)

        for i in (4, 5, 3, 6, 2, 7, 1):
            az_copy(i).start()

    for gg, (first, count) in enumerate(((0, 5), (5, 4))):
        for n in range(first, first + count):
            @pl.when((g == gg) & (b != OWNER[n]))
            def _():
                copy(
                    block, g_vm.at[y, xp, core, :, pl.ds(n * B, B)], az_s.at[0], az_r.at[n], mate
                ).wait_recv()

    def lanes_y(g2):
        return pl.ds(pl.multiple_of(896 * g2, B), 256)

    def back(x2, i):
        return lax.rem(x2 + 4 - i, 4)

    def along_x(i):
        return at(y, lax.rem(x + i, 4), z, core)

    def along_y(i):
        return at(lax.rem(y + i, 4), x, z, core)

    def second_x(i, gg):
        view = g_vm.at[y, xp, core, :, pl.ds(*X_LANES[gg])]
        return copy(view, view, a2_s.at[i], a2_r.at[i], along_x(i))

    def second_y(i):
        view = g_vm.at[y, xp, core, :, lanes_y(g)]
        return copy(view, view, a2_s.at[4 + i], a2_r.at[4 + i], along_y(i))

    def third_x(i):
        view = g_vm.at[y, :, core, :, pl.ds(*X_ALL)]
        return copy(view, view, a3_s.at[i], a3_r.at[i], along_y(i))

    def third_y(i):
        view = g_vm.at[:, xp, core, :, lanes_y(g)]
        return copy(view, view, a3_s.at[4 + i], a3_r.at[4 + i], along_x(i))

    def place_x(ref, i, c2):
        return ref.at[back(y, i), :, c2, :, pl.ds(*X_ALL)]

    def place_y(ref, i, c2):
        x2 = back(x, i)
        return ref.at[:, lax.rem(x2, 2), c2, :, lanes_y(x2 // 2)]

    def mate_x(i, c2):
        return copy(place_x(g_vm, i, c2), place_x(g_ref, i, c2), am_s.at[i], am_r.at[i], mate)

    def mate_y(i, c2):
        return copy(
            place_y(g_vm, i, c2), place_y(g_ref, i, c2), am_s.at[4 + i], am_r.at[4 + i], mate
        )

    def keep_x(i):
        return pltpu.make_async_copy(place_x(g_vm, i, core), place_x(g_ref, i, core), keep.at[i])

    def keep_y(i):
        return pltpu.make_async_copy(
            place_y(g_vm, i, core), place_y(g_ref, i, core), keep.at[4 + i]
        )

    ORDER = (1, 3, 2)
    for i in ORDER:
        for gg in range(2):
            @pl.when(g == gg)
            def _():
                second_x(i, gg).start()
        second_y(i).start()
    for i in ORDER:
        for gg in range(2):
            @pl.when(back(x, i) // 2 == gg)
            def _():
                second_x(i, gg).wait_recv()
    for i in ORDER:
        third_x(i).start()
    for i in ORDER:
        second_y(i).wait_recv()
    for i in ORDER:
        third_y(i).start()
    mate_x(0, core).start()
    keep_x(0).start()
    mate_y(0, core).start()
    keep_y(0).start()


    gtxt_ref[...] = lax.dot_general(
        grad_pre, head_ref[...], NT, preferred_element_type=jnp.float32
    ).astype(jnp.bfloat16)
    process_texts(2)
    band_wait(1, txts, 3)
    process_texts(3)
    swap_i = send(acc_i.at[pl.ds(B, B)], got_i, pair_s.at[3], pair_r.at[3], mate)
    third_x(1).wait_recv()
    mate_x(1, core).start()
    keep_x(1).start()
    third_y(1).wait_recv()
    mate_y(1, core).start()
    keep_y(1).start()
    third_x(3).wait_recv()
    mate_x(3, core).start()
    keep_x(3).start()
    third_y(3).wait_recv()
    mate_y(3, core).start()
    keep_y(3).start()
    third_x(2).wait_recv()
    mate_x(2, core).start()
    keep_x(2).start()
    third_y(2).wait_recv()
    mate_y(2, core).start()
    keep_y(2).start()
    swap_i.wait_recv()
    grad_iz = 10.0 * (acc_i[0:B] + got_i[...])
    image_g = img_ref[...].astype(jnp.float32)
    image_unit = image_g * image_inv
    gimg_ref[...] = (
        (grad_iz - image_unit * jnp.sum(image_unit * grad_iz, axis=-1, keepdims=True)) * image_inv
    ).astype(jnp.bfloat16)

    for cond, c in maybe:
        pl.when(cond)(c.wait_send)
    for kind, buf in ((0, imgs), (1, txts)):
        @pl.when(wanted(kind))
        def _():
            for n in range(PARTS[kind]):
                band_copy(kind, buf, 3, kind, n).wait_send()
    for c in sent:
        c.wait_send()

    def gp_drain(i, carry):
        gp_copy(i).wait_send()
        return carry

    lax.fori_loop(1, 16, gp_drain, 0)
    for n, to in enumerate(OWNER):
        @pl.when(b != to)
        def _():
            rs_copy(n, to).wait_send()

    @pl.when(is_owner)
    def _():
        def az_drain(i, carry):
            az_copy(i).wait_send()
            return carry

        lax.fori_loop(1, 8, az_drain, 0)

    for i in ORDER:
        for gg in range(2):
            @pl.when(g == gg)
            def _():
                second_x(i, gg).wait_send()
        second_y(i).wait_send()
        third_x(i).wait_send()
        third_y(i).wait_send()
    for i in range(4):
        keep_x(i).wait()
        keep_y(i).wait()
        mate_x(i, core).wait_send()
        mate_y(i, core).wait_send()
        mate_x(i, 1 - core).wait_recv()
        mate_y(i, 1 - core).wait_recv()


def finish(g_ref, gimg_ref, gtxt_ref, oimg_ref, otxt_ref, ohead_ref, whole):
    @pl.when(pl.program_id(0) == 0)
    def _():
        oimg_ref[...] = gimg_ref[...]
        otxt_ref[...] = gtxt_ref[...]

    for a in range(16):
        view = g_ref[a // 4, (a // 2) % 2, a % 2]
        if a % 2 == 0:
            whole[72 * a : 72 * a + 80] = view
        else:
            whole[72 * a + 8 : 72 * a + 72] = view[16:80]
    for start, size in ((0, 256), (256, 128)):
        eye = lax.broadcasted_iota(jnp.int32, (size, size), 0) == lax.broadcasted_iota(
            jnp.int32, (size, size), 1
        )
        ohead_ref[start : start + size] = lax.dot_general(
            eye.astype(jnp.bfloat16), whole[:, start : start + size], NT,
            preferred_element_type=jnp.float32,
        )


def shards(image_emb, image_ids, text_feats, text_ids, text_head):
    bf, f32 = jnp.bfloat16, jnp.float32
    vmem = pl.BlockSpec(memory_space=pltpu.VMEM)
    hbm = pl.BlockSpec(memory_space=pl.ANY)
    dma = pltpu.SemaphoreType.DMA
    scratch = [
        pltpu.VMEM((B, D), bf),
        pltpu.VMEM((B, D), bf),
        pltpu.VMEM((D, D), bf),
        pltpu.VMEM((4, 2, B, D), bf),
        pltpu.VMEM((4, 2, B, D), bf),
        pltpu.VMEM((2 * B, D), bf),
        pltpu.VMEM((2 * B, D), bf),
        pltpu.VMEM((8, 16, B), jnp.int32),
        pltpu.VMEM((2 * B, B), f32),
        pltpu.VMEM((2 * B, B), f32),
        pltpu.VMEM((2 * B, D), f32),
        pltpu.VMEM((2 * B, D), f32),
        pltpu.VMEM((B, D), f32),
        pltpu.VMEM((B, D), f32),
        pltpu.VMEM((B, D), f32),
        pltpu.VMEM((D, B), bf),
        pltpu.VMEM((4, 2, 2, B, D), bf),
        pltpu.VMEM((SLICE, 16 * B), bf),
        pltpu.VMEM((9, SLICE, B), bf),
        pltpu.VMEM((16, SLICE, B), bf),
        pltpu.VMEM((SLICE, B), bf),
        dma((3,)),
    ]
    for n in (48, 7, 4, 21, 16):
        scratch += [dma((n,)), dma((n,))]
    scratch += [dma((9,)), dma((16,)), dma((8,)), dma((9,))]
    for n in (8, 8, 8):
        scratch += [dma((n,)), dma((n,))]
    scratch += [pltpu.VMEM((4, 2, 2, SLICE, D), bf), dma((8,))]
    gimg, gtxt, g = pl.pallas_call(
        kernel,
        out_shape=(
            jax.ShapeDtypeStruct((B, D), bf),
            jax.ShapeDtypeStruct((B, D), bf),
            jax.ShapeDtypeStruct((4, 2, 2, SLICE, D), bf),
        ),
        in_specs=[hbm, vmem, hbm, vmem, hbm],
        out_specs=(vmem, vmem, hbm),
        scratch_shapes=scratch,
        compiler_params=pltpu.CompilerParams(
            collective_id=0, has_side_effects=True, vmem_limit_bytes=60 * 2**20
        ),
    )(image_emb, image_ids.reshape(1, B), text_feats, text_ids.reshape(1, B), text_head)
    fixed = pl.BlockSpec((B, D), lambda n: (0, 0))
    return pl.pallas_call(
        finish,
        grid=(D // WIDE,),
        out_shape=(
            jax.ShapeDtypeStruct((B, D), bf),
            jax.ShapeDtypeStruct((B, D), bf),
            jax.ShapeDtypeStruct((D, D), f32),
        ),
        in_specs=[pl.BlockSpec((4, 2, 2, SLICE, WIDE), lambda n: (0, 0, 0, 0, n)), fixed, fixed],
        out_specs=(fixed, fixed, pl.BlockSpec((WIDE, D), lambda n: (n, 0))),
        scratch_shapes=[pltpu.VMEM((D, WIDE), bf)],
        compiler_params=pltpu.CompilerParams(vmem_limit_bytes=60 * 2**20),
    )(g, gimg, gtxt)


def solution(mesh):
    placed = (P("blk", None), P("blk"), P("blk", None), P("blk"), P())
    return jax.shard_map(
        shards,
        mesh=mesh,
        in_specs=placed,
        out_specs=(P("blk", None), P("blk", None), P()),
        check_vma=False,
    )
```
